32 devices in a mesh: rep: 4 (over y, x), seq: 8 (over z, core).
Axes of the slice: x: 2, y: 2, z: 4, core: 2. Of those that a mesh axis runs over, the one named last changes fastest.
Arguments:
- queries: bfloat16 [4, 1024, 3072], P('rep', 'seq'), may hold values from -6 to 6
- keys: bfloat16 [4, 1024, 128], P('rep', 'seq'), may hold values from -6 to 6
- values: bfloat16 [4, 1024, 128], P('rep', 'seq'), may hold values from -6 to 6
- outputs: bfloat16 [4, 1024, 3072], P('rep', 'seq'), may hold values from -6 to 6
- out_grad: bfloat16 [4, 1024, 3072], P('rep', 'seq'), may hold values from -24 to 24
- log_norm: float32 [4, 24, 1024], P('rep', None, 'seq'), may hold values from 7 to 8.5
- inputs: bfloat16 [4, 1024, 6144], P('rep', 'seq'), may hold values from -0.29882812 to 0.29882812
- mlp_weight: bfloat16 [4, 12288, 6144], P('rep', 'seq'), may hold values from -0.0546875 to 0.0546875
- initial_right_factor: bfloat16 [8, 4, 6144], P('seq'), may hold values from -6 to 6
Outputs:
- query_grad: float32 [4, 1024, 3072], P('rep', 'seq')
- kv_grad: float32 [4, 1024, 256], P('rep', 'seq')
- proj_grad: float32 [4, 6144, 256], P('rep', 'seq')
- left_factor: float32 [4, 2, 4, 12288], P('rep', None, None, 'seq')
- right_factor: float32 [4, 8, 2, 4, 6144], P('rep', 'seq')
The draws below stay inside these ranges and needn't reach their ends.
All inputs are finite; a program needn't handle non-finite values.
Results may differ from the reference program's by a relative error of at most 0.004.
Values may be sent and summed in bfloat16 or wider, within the bound.
No kernel may reach another device: no remote copies, remote signals or barrier semaphores. Data moves between devices by JAX's collectives and lax.ppermute only.
A program may use at most 128 MiB of HBM per device.

```python
import jax
import jax.numpy as jnp
from jax import lax

D = 6144
HEADS = 24
HD = 128
FF = 12288
WINDOW = 2048
RANK = 4
TOK_DEV = 128
SEQUENCE_LENGTH = 1024
BLOCK_ROWS = 1536
N_REP = 4
N_SEQ = 8


def spiked(values, stream_key, source, target, blocks, factor):
    def block_of(dim):
        return (jnp.arange(values.shape[dim]) // (values.shape[dim] // blocks)).reshape((-1,) + (1,) * (values.ndim - 1 - dim))

    one_side = jax.random.permutation(stream_key, blocks)[block_of(target)]
    far = (block_of(target) + blocks // 2) % blocks
    return jnp.where((block_of(source) == one_side) | (block_of(source) == far), factor * values, values)


def levels(own_key, extent, shards, smallest, high):
    factor_of = 1.0
    for position, parts in shards:
        draws = jax.random.uniform(jax.random.fold_in(jax.random.fold_in(own_key, 6), position), (parts,), jnp.float32, smallest / len(shards), high / len(shards))
        factor_of = factor_of * jnp.repeat(jnp.exp(draws), extent[position] // parts).reshape((-1,) + (1,) * (len(extent) - 1 - position))
    return factor_of


def normal_values(key, dims, deviation, bound, cuts=(), held_as=jnp.bfloat16):
    gain = levels(key, dims, cuts, -0.22, 0.18) if cuts else 1.0
    drawn = jax.random.normal(key, dims, jnp.float32) * deviation * gain
    return jnp.minimum(jnp.maximum(drawn, -bound), bound).astype(held_as)


def heavy_noise(rng, shape, spread, limit, pieces, heavy, held_as=jnp.bfloat16):
    entries = spread * jax.random.normal(rng, shape, jnp.float32)
    if pieces:
        entries = entries * levels(rng, shape, pieces, -0.22, 0.18)
    return jnp.clip(spiked(entries, jax.random.fold_in(rng, 3), *heavy), -limit, limit).astype(held_as)


def setup_inputs(seed: int = 0) -> dict:
    seeds = jax.random.split(jax.random.key(seed), 10)
    queries = normal_values(seeds[0], (N_REP, SEQUENCE_LENGTH, HEADS * HD), 1.0, 6.0, ((0, 4), (1, 8)))
    keys = normal_values(seeds[1], (N_REP, SEQUENCE_LENGTH, HD), 1.0, 6.0, ((0, 4), (1, 8)))
    values = normal_values(seeds[2], (N_REP, SEQUENCE_LENGTH, HD), 1.0, 6.0, ((0, 4), (1, 8)))
    outputs = normal_values(seeds[3], (N_REP, SEQUENCE_LENGTH, HEADS * HD), 1.0, 6.0, ((0, 4), (1, 8)))
    out_grad = normal_values(seeds[4], (N_REP, SEQUENCE_LENGTH, HEADS * HD), 4.0, 24.0, ((0, 4), (1, 8)))
    log_norm = jnp.clip(7.0 + 1.5 * jax.random.uniform(seeds[5], (N_REP, HEADS, SEQUENCE_LENGTH), jnp.float32) ** levels(seeds[5], (N_REP, HEADS, SEQUENCE_LENGTH), ((0, 4), (2, 8)), -0.2, 0.2), 7.0, 8.5)
    inputs = heavy_noise(seeds[6], (N_REP, SEQUENCE_LENGTH, D), 0.05, 0.29882812, ((0, 4), (1, 8)), (1, 2, 8, 2.0))
    mlp_weight = normal_values(seeds[7], (N_REP, FF, D), FF ** -0.5, 0.0546875, ((0, 4), (1, 8)))
    initial_right_factor = normal_values(seeds[8], (N_SEQ, RANK, D), 1.0, 6.0, ((0, 8),))
    return {"queries": queries, "keys": keys, "values": values, "outputs": outputs, "out_grad": out_grad, "log_norm": log_norm, "inputs": inputs, "mlp_weight": mlp_weight, "initial_right_factor": initial_right_factor}


epsilon = 1e-06

def window_mask(first_query, row_count, span):
    query_pos = first_query + jnp.arange(row_count, dtype=jnp.int32)
    key_pos = first_query - span + jnp.arange(span + row_count, dtype=jnp.int32)
    lower_ok = key_pos[None, :] > query_pos[:, None] - span
    upper_ok = key_pos[None, :] <= query_pos[:, None]
    return (key_pos[None, :] >= 0) & lower_ok & upper_ok

def attend(query_blk, gradient_block, out_blk, norm_block, window_kv, visible, scale):
    row_count, model_cols = query_blk.shape
    head_count = norm_block.shape[0]
    width = model_cols // head_count
    group = 8 if head_count % 8 == 0 else head_count
    groups = head_count // group

    def head_rows(source):
        return source.reshape(row_count, head_count, width).transpose(1, 0, 2).reshape(groups, group * row_count, width)
    query_rows = head_rows(query_blk)
    grad_rows = head_rows(gradient_block)
    delta_all = lax.optimization_barrier(jnp.sum(gradient_block.astype(jnp.float32).reshape(row_count, head_count, width) * out_blk.astype(jnp.float32).reshape(row_count, head_count, width), axis=-1))
    delta_rows = delta_all.T.reshape(groups, group * row_count)
    norm_rows = norm_block.reshape(groups, group, row_count)
    key_mat = window_kv[:, :width]
    value_mat = window_kv[:, width:]

    def per_group(accum, items):
        query_grp, grad_grp, norm_grp, delta_grp = items
        scores = jnp.dot(query_grp, key_mat.T, preferred_element_type=jnp.float32) * scale
        scores = scores.reshape(group, row_count, -1)
        probs = jnp.where(visible[None], jnp.exp(scores - norm_grp[:, :, None]), 0.0)
        probs = probs.reshape(group * row_count, -1)
        probs_b = probs.astype(jnp.bfloat16)
        value_grad = jnp.dot(probs_b.T, grad_grp, preferred_element_type=jnp.float32)
        prob_grad = jnp.dot(grad_grp, value_mat.T, preferred_element_type=jnp.float32)
        score_grad = (scale * probs * (prob_grad - delta_grp[:, None])).astype(jnp.bfloat16)
        query_grad = jnp.dot(score_grad, key_mat, preferred_element_type=jnp.float32)
        key_grad = jnp.dot(score_grad.T, query_grp, preferred_element_type=jnp.float32)
        return (accum + jnp.concatenate([key_grad, value_grad], axis=-1), query_grad)
    start_accum = jnp.zeros((window_kv.shape[0], 2 * width), jnp.float32)
    accum, query_grads = lax.scan(per_group, start_accum, (query_rows, grad_rows, norm_rows, delta_rows))
    query_grad = query_grads.reshape(head_count, row_count, width).transpose(1, 0, 2).reshape(row_count, model_cols)
    return (query_grad, accum)

def orthonormal(diffs):
    columns = []
    for index in range(diffs.shape[-2]):
        source = diffs[..., index, :]
        vector = source
        for previous in columns:
            vector = vector - lax.optimization_barrier(jnp.mean(source * previous, axis=-1, keepdims=True)) * previous
        columns.append(vector * lax.rsqrt(lax.optimization_barrier(jnp.mean(vector * vector, axis=-1, keepdims=True)) + epsilon))
    return jnp.stack(columns, axis=-2)

def reference(queries, keys, values, outputs, out_grad, log_norm, inputs, mlp_weight, initial_right_factor):
    scale = HD ** (-0.5)

    def single_replica(items):
        query_matrix, key_all, value_all, out_all, grad_all, norm_all, input_all = items
        joined = jnp.concatenate([key_all, value_all], axis=-1)
        padded = jnp.concatenate([jnp.zeros((WINDOW, 2 * HD), joined.dtype), joined], axis=0)

        def one_block(accum, block_index):
            first = block_index * TOK_DEV
            window_kv = lax.dynamic_slice_in_dim(padded, first, WINDOW + TOK_DEV, 0)
            query_blk = lax.dynamic_slice_in_dim(query_matrix, first, TOK_DEV, 0)
            gradient_block = lax.dynamic_slice_in_dim(grad_all, first, TOK_DEV, 0)
            out_blk = lax.dynamic_slice_in_dim(out_all, first, TOK_DEV, 0)
            norm_block = lax.dynamic_slice_in_dim(norm_all, first, TOK_DEV, 1)
            visible = window_mask(first, TOK_DEV, WINDOW)
            query_grad, window_grads = attend(query_blk, gradient_block, out_blk, norm_block, window_kv, visible, scale)
            current = lax.dynamic_slice_in_dim(accum, first, WINDOW + TOK_DEV, 0)
            accum = lax.dynamic_update_slice_in_dim(accum, current + window_grads, first, 0)
            return (accum, query_grad)
        start_accum = jnp.zeros((WINDOW + SEQUENCE_LENGTH, 2 * HD), jnp.float32)
        accum, query_grads = lax.scan(one_block, start_accum, jnp.arange(N_SEQ, dtype=jnp.int32))
        kv_grad = accum[WINDOW:]
        proj_grad = jnp.dot(input_all.T, kv_grad.astype(jnp.bfloat16), preferred_element_type=jnp.float32)
        return (query_grads.reshape(SEQUENCE_LENGTH, HEADS * HD), kv_grad, proj_grad)
    query_grad, kv_grad, proj_grad = lax.map(single_replica, (queries, keys, values, outputs, out_grad, log_norm, inputs))
    blocks = mlp_weight.reshape(N_REP, N_SEQ, BLOCK_ROWS, D)

    def project(weight_row_blocks):
        return jnp.einsum('chi,cei->che', initial_right_factor.astype(jnp.float32), weight_row_blocks.astype(jnp.float32))
    acts = lax.map(project, blocks)
    lower_diff = acts - jnp.roll(acts, 1, axis=0)
    higher_diff = acts - jnp.roll(acts, -1, axis=0)
    diffs = jnp.stack([lower_diff, higher_diff], axis=2)
    basis = orthonormal(diffs)
    left_factor = basis.transpose(0, 2, 3, 1, 4).reshape(N_REP, 2, RANK, FF)
    basis_b = basis.astype(jnp.bfloat16)

    def contract(items):
        basis_rep, weight_row_blocks = items
        return jnp.einsum('bekr,brd->bekd', basis_rep.astype(jnp.float32), weight_row_blocks.astype(jnp.float32))
    contrib = lax.map(contract, (basis_b, blocks))
    lower_edge = contrib[:, :, 0] + jnp.roll(contrib[:, :, 1], 1, axis=0)
    higher_edge = contrib[:, :, 1] + jnp.roll(contrib[:, :, 0], -1, axis=0)
    right_factor = jnp.stack([lower_edge, higher_edge], axis=2)
    return (query_grad, kv_grad, proj_grad, left_factor, right_factor)
```

```python
import functools
import math

import jax
import jax.numpy as jnp
from jax import lax
from jax.experimental import pallas as pl
from jax.experimental.pallas import tpu as pltpu
from jax.sharding import PartitionSpec as P

WINDOW = 2048
EPSILON = 1e-06
LOG2E = math.log2(math.e)
F32 = jnp.float32
BF16 = jnp.bfloat16
VMEM_LIMIT = 48 * 1024 * 1024


def dot_nt(a, b):
    return lax.dot_general(a, b, (((1,), (1,)), ((), ())), preferred_element_type=F32)


def dot_tn(a, b):
    return lax.dot_general(a, b, (((0,), (0,)), ((), ())), preferred_element_type=F32)


def vmem_specs(count):
    return [pl.BlockSpec(memory_space=pltpu.VMEM)] * count


def delta_kernel(head_dim, grad_ref, out_ref, delta_ref):
    for head in range(delta_ref.shape[0]):
        cols = slice(head * head_dim, (head + 1) * head_dim)
        prod = grad_ref[:, cols].astype(F32) * out_ref[:, cols].astype(F32)
        delta_ref[head : head + 1, :] = jnp.sum(prod.T, axis=0, keepdims=True)


def head_delta(out_grad, outputs, heads):
    rows, cols = out_grad.shape
    return pl.pallas_call(
        functools.partial(delta_kernel, cols // heads),
        out_shape=jax.ShapeDtypeStruct((heads, rows), F32),
        in_specs=vmem_specs(2),
        out_specs=pl.BlockSpec(memory_space=pltpu.VMEM),
        compiler_params=pltpu.CompilerParams(vmem_limit_bytes=VMEM_LIMIT),
        cost_estimate=pl.CostEstimate(
            flops=2 * rows * cols, bytes_accessed=4 * rows * cols, transcendentals=0
        ),
    )(out_grad, outputs)


def attention_kernel(blocks, group, scale, me_ref, q_ref, do_ref, norm_ref, delta_ref, *refs):
    kv_refs = refs[:blocks]
    qg_ref = refs[blocks]
    grad_refs = refs[blocks + 1 : 2 * blocks + 1]
    acc_ref, kt_ref, qgt_ref = refs[2 * blocks + 1 :]
    tok = q_ref.shape[0]
    span, hd = kv_refs[0].shape[0], kv_refs[0].shape[1] // 2
    heads = norm_ref.shape[0]
    me = me_ref[0]
    acc_ref[...] = jnp.zeros_like(acc_ref)
    for k in range(blocks):
        kt_ref[k] = kv_refs[k][:, :hd].T

    def step(index, carry):
        def stacked(ref):
            parts = []
            for i in range(group):
                first = pl.multiple_of((index * group + i) * hd, hd)
                parts.append(ref[:, pl.ds(first, hd)])
            return jnp.concatenate(parts, axis=0)

        def row(ref):
            return jnp.concatenate(
                [ref[pl.ds(index * group + i, 1), :] for i in range(group)], axis=1
            )

        q = stacked(q_ref)
        do = stacked(do_ref)
        norm = row(norm_ref) * LOG2E
        delta = row(delta_ref)
        qgt = None
        for k in range(blocks):
            key = kv_refs[k][:, :hd]
            value = kv_refs[k][:, hd:]
            probs = jnp.exp2(dot_nt(key, q) * (scale * LOG2E) - norm)
            if k == 0 or (k + 1) * span > WINDOW:
                shape = probs.shape
                key_pos = (me // 2 - k) * span + lax.broadcasted_iota(jnp.int32, shape, 0)
                query = lax.broadcasted_iota(jnp.int32, shape, 1)
                query_pos = me * tok + lax.rem(query, tok)
                visible = (key_pos <= query_pos) & (key_pos > query_pos - WINDOW)
                probs = jnp.where(visible, probs, 0.0)
            prob_grad = dot_nt(value, do)
            score_grad = (scale * probs * (prob_grad - delta)).astype(BF16)
            acc_ref[k, :, hd:] += jnp.dot(probs.astype(BF16), do, preferred_element_type=F32)
            acc_ref[k, :, :hd] += jnp.dot(score_grad, q, preferred_element_type=F32)
            part = jnp.dot(kt_ref[k], score_grad, preferred_element_type=F32)
            qgt = part if qgt is None else qgt + part
        qgt_ref[...] = qgt
        for i in range(group):
            first = pl.multiple_of((index * group + i) * hd, hd)
            qg_ref[:, pl.ds(first, hd)] = qgt_ref[:, i * tok : (i + 1) * tok].T
        return carry

    lax.fori_loop(0, heads // group, step, 0)
    for k in range(blocks):
        grad_refs[k][...] = acc_ref[k].astype(grad_refs[k].dtype)


def attend(me, queries, out_grad, norm, delta, kvs):
    tok, cols = queries.shape
    heads = norm.shape[0]
    hd = cols // heads
    span = kvs[0].shape[0]
    blocks = len(kvs)
    group = next(g for g in (4, 3, 2, 1) if heads % g == 0)
    outs = [jax.ShapeDtypeStruct((tok, cols), F32), jax.ShapeDtypeStruct((span, 2 * hd), F32)]
    outs += [jax.ShapeDtypeStruct((span, 2 * hd), BF16)] * (blocks - 1)
    work = heads * tok * span * blocks
    return pl.pallas_call(
        functools.partial(attention_kernel, blocks, group, hd ** (-0.5)),
        out_shape=outs,
        in_specs=[pl.BlockSpec(memory_space=pltpu.SMEM)] + vmem_specs(4 + blocks),
        out_specs=vmem_specs(len(outs)),
        scratch_shapes=[
            pltpu.VMEM((blocks, span, 2 * hd), F32),
            pltpu.VMEM((blocks, hd, span), BF16),
            pltpu.VMEM((hd, group * tok), F32),
        ],
        compiler_params=pltpu.CompilerParams(vmem_limit_bytes=VMEM_LIMIT),
        cost_estimate=pl.CostEstimate(
            flops=20 * work * hd, bytes_accessed=8 * tok * cols, transcendentals=work
        ),
    )(me[None], queries, out_grad, norm, delta, *kvs)


def project_kernel(chips, me_ref, x_ref, *refs):
    grad_refs, out_ref = refs[:chips], refs[chips]
    tok, width = x_ref.shape[1:]
    chip = me_ref[0] // 2
    total = None
    for k in range(chips):
        source = lax.rem(chip - k + chips, chips)
        x = x_ref[pl.ds(2 * source, 2)].reshape(2 * tok, width)
        part = dot_tn(x, grad_refs[k][...])
        total = part if total is None else total + part
    out_ref[...] = total


def project(me, blocks, grads):
    count, tok, width = blocks.shape
    cols = grads[0].shape[1]
    return pl.pallas_call(
        functools.partial(project_kernel, len(grads)),
        out_shape=jax.ShapeDtypeStruct((width, cols), F32),
        in_specs=[pl.BlockSpec(memory_space=pltpu.SMEM)] + vmem_specs(1 + len(grads)),
        out_specs=pl.BlockSpec(memory_space=pltpu.VMEM),
        compiler_params=pltpu.CompilerParams(vmem_limit_bytes=VMEM_LIMIT),
        cost_estimate=pl.CostEstimate(
            flops=2 * count * tok * width * cols,
            bytes_accessed=2 * count * tok * width,
            transcendentals=0,
        ),
    )(me[None], blocks, *grads)


def orthonormal(diffs):
    columns = []
    for index in range(diffs.shape[-2]):
        source = diffs[..., index, :]
        vector = source
        for previous in columns:
            vector = vector - jnp.mean(source * previous, axis=-1, keepdims=True) * previous
        columns.append(
            vector * lax.rsqrt(jnp.mean(vector * vector, axis=-1, keepdims=True) + EPSILON)
        )
    return jnp.stack(columns, axis=-2)


def from_cycle(block, axis, distance):
    count = lax.axis_size(axis)
    return lax.ppermute(block, axis, [(i, (i + distance) % count) for i in range(count)])


def from_line(block, axis, distance):
    count = lax.axis_size(axis)
    route = [(i, i + distance) for i in range(count) if 0 <= i + distance < count]
    return lax.ppermute(block, axis, route)


def from_partner(block, axis):
    count = lax.axis_size(axis)
    return lax.ppermute(block, axis, [(i, i ^ 1) for i in range(count)])


def on_device(
    queries, keys, values, outputs, out_grad, log_norm, inputs, mlp_weight, initial_right_factor
):
    tok = queries.shape[1]
    heads = log_norm.shape[1]
    count = lax.axis_size("seq")
    chips = count // 2
    me = lax.axis_index("seq")
    odd = lax.rem(me, 2) == 1
    reach = min(chips - 1, -(-WINDOW // (2 * tok)))

    own_kv = jnp.concatenate([keys[0], values[0]], axis=-1)
    other_kv = from_partner(own_kv, "seq")
    chip_kv = jnp.concatenate(
        [jnp.where(odd, other_kv, own_kv), jnp.where(odd, own_kv, other_kv)], axis=0
    )
    kvs = [chip_kv] + [from_line(chip_kv, "seq", 2 * k) for k in range(1, reach + 1)]

    width = inputs.shape[2] // count
    split_inputs = inputs[0].reshape(tok, count, width).transpose(1, 0, 2)
    split_inputs, kvs = lax.optimization_barrier((split_inputs, kvs))
    feature_blocks = lax.all_to_all(
        split_inputs, "seq", split_axis=0, concat_axis=0, tiled=True
    )

    delta = head_delta(out_grad[0], outputs[0], heads)
    query_grad, chip_grad, *sent = attend(me, queries[0], out_grad[0], log_norm[0], delta, kvs)
    for k, part in enumerate(sent, 1):
        chip_grad = chip_grad + from_line(part, "seq", -2 * k).astype(F32)
    chip_grad = chip_grad + from_partner(chip_grad, "seq")
    own_grad = jnp.where(odd, chip_grad[tok:], chip_grad[:tok])
    chip_grad_b = chip_grad.astype(BF16)
    grads = [chip_grad_b] + [from_cycle(chip_grad_b, "seq", 2 * k) for k in range(1, chips)]
    proj_grad = project(me, feature_blocks, grads)

    weight_block = mlp_weight[0]
    acts = jnp.einsum(
        "kd,rd->kr", initial_right_factor[0], weight_block, preferred_element_type=F32
    )
    lower_acts = from_cycle(acts, "rep", 1)
    higher_acts = from_cycle(acts, "rep", -1)
    basis = orthonormal(jnp.stack([acts - lower_acts, acts - higher_acts], axis=0))
    contrib = jnp.einsum(
        "ekr,rd->ekd", basis.astype(BF16), weight_block, preferred_element_type=F32
    )
    lower_half = from_cycle(contrib[1], "rep", 1)
    higher_half = from_cycle(contrib[0], "rep", -1)
    right_factor = jnp.stack([contrib[0] + lower_half, contrib[1] + higher_half], axis=0)
    return (
        query_grad[None],
        own_grad[None],
        proj_grad[None],
        basis[None],
        right_factor[None, None],
    )


def solution(mesh):
    return jax.shard_map(
        on_device,
        mesh=mesh,
        in_specs=(
            P("rep", "seq", None),
            P("rep", "seq", None),
            P("rep", "seq", None),
            P("rep", "seq", None),
            P("rep", "seq", None),
            P("rep", None, "seq"),
            P("rep", "seq", None),
            P("rep", "seq", None),
            P("seq", None, None),
        ),
        out_specs=(
            P("rep", "seq", None),
            P("rep", "seq", None),
            P("rep", "seq", None),
            P("rep", None, None, "seq"),
            P("rep", "seq", None, None, None),
        ),
        check_vma=False,
    )
```

```python
import functools
import math

import jax
import jax.numpy as jnp
from jax import lax
from jax.experimental import pallas as pl
from jax.experimental.pallas import tpu as pltpu
from jax.sharding import PartitionSpec as P

WINDOW = 2048
EPSILON = 1e-06
LOG2E = math.log2(math.e)
F32 = jnp.float32
BF16 = jnp.bfloat16
VMEM_LIMIT = 48 * 1024 * 1024
PARTS = 3
PARTS = 3
COST = pl.CostEstimate(flops=1, bytes_accessed=1, transcendentals=0)


def dot_nt(a, b):
    return lax.dot_general(a, b, (((1,), (1,)), ((), ())), preferred_element_type=F32)


def dot_tn(a, b):
    return lax.dot_general(a, b, (((0,), (0,)), ((), ())), preferred_element_type=F32)


def vmem_specs(count):
    return [pl.BlockSpec(memory_space=pltpu.VMEM)] * count


def delta_kernel(head_dim, grad_ref, out_ref, delta_ref):
    for head in range(delta_ref.shape[0]):
        cols = slice(head * head_dim, (head + 1) * head_dim)
        prod = grad_ref[:, cols].astype(F32) * out_ref[:, cols].astype(F32)
        delta_ref[head : head + 1, :] = jnp.sum(prod.T, axis=0, keepdims=True)


def head_delta(out_grad, outputs, heads):
    rows, cols = out_grad.shape
    return pl.pallas_call(
        functools.partial(delta_kernel, cols // heads),
        out_shape=jax.ShapeDtypeStruct((heads, rows), F32),
        in_specs=vmem_specs(2),
        out_specs=pl.BlockSpec(memory_space=pltpu.VMEM),
        compiler_params=pltpu.CompilerParams(vmem_limit_bytes=VMEM_LIMIT),
        cost_estimate=COST,
    )(out_grad, outputs)


def swap(block, axis, bit, only_up=None):
    count = lax.axis_size(axis)
    route = [
        (i, i ^ bit) for i in range(count) if only_up is None or (i < i ^ bit) == only_up
    ]
    return lax.ppermute(block, axis, route)


def gather_bits(count):
    return [1 << b for b in reversed(range(count.bit_length() - 1))]


def gather_order(count):
    order = [0]
    for bit in gather_bits(count):
        order = order + [x ^ bit for x in order]
    return order


def swap(block, axis, bit, only_up=None):
    count = lax.axis_size(axis)
    route = [
        (i, i ^ bit) for i in range(count) if only_up is None or (i < i ^ bit) == only_up
    ]
    return lax.ppermute(block, axis, route)


def gather_bits(count):
    return [1 << b for b in reversed(range(count.bit_length() - 1))]


def gather_order(count):
    order = [0]
    for bit in gather_bits(count):
        order = order + [x ^ bit for x in order]
    return order


def attention_kernel(
    order, group, join, scale, me_ref, q_ref, do_ref, norm_ref, delta_ref, near_ref, far_ref,
    qg_ref, near_grad_ref, far_grad_ref, near_t_ref, far_t_ref, qgt_ref,
):
    tok = q_ref.shape[0]
    hd = near_ref.shape[1] // 2
    heads = norm_ref.shape[0]
    half = near_ref.shape[0]
    rows = join * tok
    me = me_ref[0]
    windowed = len(order) * tok > WINDOW
    chunks = [(s, first) for s in range(2) for first in range(0, half, rows)]
    kv_refs = (near_ref, far_ref)
    grad_refs = (near_grad_ref, far_grad_ref)
    t_refs = (near_t_ref, far_t_ref)
    for s, first in chunks:
        t_refs[s][:, first : first + rows] = kv_refs[s][first : first + rows, :hd].T
        grad_refs[s][first : first + rows, :] = jnp.zeros((rows, 2 * hd), F32)

    def step(index, carry):
        def stacked(ref):
            parts = []
            for i in range(group):
                first = pl.multiple_of((index * group + i) * hd, hd)
                parts.append(ref[:, pl.ds(first, hd)])
            return jnp.concatenate(parts, axis=0)

        def row(ref):
            return jnp.concatenate(
                [ref[pl.ds(index * group + i, 1), :] for i in range(group)], axis=1
            )

        q = stacked(q_ref)
        do = stacked(do_ref)
        norm = row(norm_ref) * LOG2E
        delta = row(delta_ref)
        qgt = None
        for s, first in chunks:
            area = slice(first, first + rows)
            key = kv_refs[s][area, :hd]
            value = kv_refs[s][area, hd:]
            logits = dot_nt(key, q) * (scale * LOG2E)
            parts = []
            for j in range(join):
                x = order[(s * half + first) // tok + j]
                source = me ^ x
                part = logits[j * tok : (j + 1) * tok]
                if x == 0 or windowed:
                    key_pos = source * tok + lax.broadcasted_iota(jnp.int32, part.shape, 0)
                    query = lax.broadcasted_iota(jnp.int32, part.shape, 1)
                    query_pos = me * tok + lax.rem(query, tok)
                    visible = (key_pos <= query_pos) & (key_pos > query_pos - WINDOW)
                    parts.append(jnp.where(visible, jnp.exp2(part - norm), 0.0))
                else:
                    hidden = jnp.where(source < me, 0.0, 1e30).astype(F32)
                    parts.append(jnp.exp2(part - (norm + hidden)))
            probs = jnp.concatenate(parts, axis=0)
            prob_grad = dot_nt(value, do)
            score_grad = (scale * probs * (prob_grad - delta)).astype(BF16)
            grad_refs[s][area, hd:] += jnp.dot(
                probs.astype(BF16), do, preferred_element_type=F32
            )
            grad_refs[s][area, :hd] += jnp.dot(score_grad, q, preferred_element_type=F32)
            part = jnp.dot(t_refs[s][:, area], score_grad, preferred_element_type=F32)
            qgt = part if qgt is None else qgt + part
        qgt_ref[...] = qgt
        for i in range(group):
            first = pl.multiple_of((index * group + i) * hd, hd)
            qg_ref[:, pl.ds(first, hd)] = qgt_ref[:, i * tok : (i + 1) * tok].T
        return carry

    lax.fori_loop(0, heads // group, step, 0)


def attend(me, queries, out_grad, norm, delta, near, far):
    tok, cols = queries.shape
    heads = norm.shape[0]
    hd = cols // heads
    half = near.shape[0]
    order = gather_order(2 * half // tok)
    group = next(g for g in (4, 3, 2, 1) if heads % g == 0)
    join = 2 if half % (2 * tok) == 0 else 1
    work = heads * tok * half * 2
    return pl.pallas_call(
        functools.partial(attention_kernel, order, group, join, hd ** (-0.5)),
        out_shape=[
            jax.ShapeDtypeStruct((tok, cols), F32),
            jax.ShapeDtypeStruct((half, 2 * hd), F32),
            jax.ShapeDtypeStruct((half, 2 * hd), F32),
        ],
        in_specs=[pl.BlockSpec(memory_space=pltpu.SMEM)] + vmem_specs(6),
        out_specs=vmem_specs(3),
        scratch_shapes=[
            pltpu.VMEM((hd, half), BF16),
            pltpu.VMEM((hd, half), BF16),
            pltpu.VMEM((hd, group * tok), F32),
        ],
        compiler_params=pltpu.CompilerParams(vmem_limit_bytes=VMEM_LIMIT),
        cost_estimate=pl.CostEstimate(
            flops=20 * work * hd, bytes_accessed=8 * tok * cols, transcendentals=work
        ),
    )(me[None], queries, out_grad, norm, delta, near, far)


def pack_kernel(x_ref, out_ref):
    width = out_ref.shape[2]
    for j in range(out_ref.shape[0]):
        out_ref[j] = x_ref[:, j * width : (j + 1) * width]


def pack(inputs, count):
    tok, cols = inputs.shape
    width = cols // count
    if width % 128:
        return inputs.reshape(tok, count, width).transpose(1, 0, 2)
    return pl.pallas_call(
        pack_kernel,
        out_shape=jax.ShapeDtypeStruct((count, tok, width), inputs.dtype),
        in_specs=vmem_specs(1),
        out_specs=pl.BlockSpec(memory_space=pltpu.VMEM),
        compiler_params=pltpu.CompilerParams(vmem_limit_bytes=VMEM_LIMIT),
        cost_estimate=pl.CostEstimate(
            flops=0, bytes_accessed=4 * tok * cols, transcendentals=0
        ),
    )(inputs)


def project_kernel(order, me_ref, x_ref, near_ref, far_ref, out_ref):
    me = me_ref[0]
    x = jnp.concatenate([x_ref[me ^ part] for part in order], axis=0)
    grads = jnp.concatenate([near_ref[...], far_ref[...]], axis=0)
    out_ref[...] = dot_tn(x, grads)


def project(me, blocks, near, far):
    count, tok, width = blocks.shape
    cols = near.shape[1]
    return pl.pallas_call(
        functools.partial(project_kernel, gather_order(count)),
        out_shape=jax.ShapeDtypeStruct((width, cols), F32),
        in_specs=[pl.BlockSpec(memory_space=pltpu.SMEM)] + vmem_specs(3),
        out_specs=pl.BlockSpec(memory_space=pltpu.VMEM),
        compiler_params=pltpu.CompilerParams(vmem_limit_bytes=VMEM_LIMIT),
        cost_estimate=pl.CostEstimate(
            flops=2 * count * tok * width * cols,
            bytes_accessed=2 * count * tok * width,
            transcendentals=0,
        ),
    )(me[None], blocks, near, far)


def acts_kernel(factor_ref, w_ref, out_ref):
    rank, rows = out_ref.shape
    part = dot_nt(w_ref[...], factor_ref[...])
    wide = jnp.concatenate([part, jnp.zeros((rows, 128 - rank), F32)], axis=1)
    out_ref[...] = wide.T[:rank]


def acts_part(factor, weight, index, parts):
    rank, cols = factor.shape
    rows = weight.shape[0] // parts
    tile = 256 if rows % 256 == 0 else rows
    steps = rows // tile
    return pl.pallas_call(
        acts_kernel,
        grid=(steps,),
        out_shape=jax.ShapeDtypeStruct((rank, rows), F32),
        in_specs=[
            pl.BlockSpec((rank, cols), lambda i: (0, 0)),
            pl.BlockSpec((tile, cols), lambda i: (index * steps + i, 0)),
        ],
        out_specs=pl.BlockSpec((rank, tile), lambda i: (0, i)),
        compiler_params=pltpu.CompilerParams(vmem_limit_bytes=VMEM_LIMIT),
        cost_estimate=pl.CostEstimate(
            flops=2 * rank * rows * cols, bytes_accessed=2 * rows * cols, transcendentals=0
        ),
    )(factor, weight)


def orthonormal(diffs):
    columns = []
    for index in range(diffs.shape[0]):
        source = diffs[index : index + 1]
        vector = source
        for previous in columns:
            vector = vector - jnp.mean(source * previous, axis=-1, keepdims=True) * previous
        columns.append(
            vector * lax.rsqrt(jnp.mean(vector * vector, axis=-1, keepdims=True) + EPSILON)
        )
    return jnp.concatenate(columns, axis=0)


def basis_kernel(acts_ref, lower_ref, higher_ref, basis_ref, both_ref):
    acts = acts_ref[...]
    edges = [orthonormal(acts - ref[...]) for ref in (lower_ref, higher_ref)]
    for e, edge in enumerate(edges):
        basis_ref[e] = edge
    both_ref[...] = jnp.concatenate(edges, axis=0).astype(BF16)


def make_basis(acts, lower, higher):
    rank, rows = acts.shape
    return pl.pallas_call(
        basis_kernel,
        out_shape=[
            jax.ShapeDtypeStruct((2, rank, rows), F32),
            jax.ShapeDtypeStruct((2 * rank, rows), BF16),
        ],
        in_specs=vmem_specs(3),
        out_specs=vmem_specs(2),
        cost_estimate=pl.CostEstimate(
            flops=60 * rank * rows, bytes_accessed=40 * rank * rows, transcendentals=0
        ),
    )(acts, lower, higher)


def contrib_kernel(both_ref, w_ref, out_ref):
    rank = out_ref.shape[1]
    part = jnp.dot(both_ref[...], w_ref[...], preferred_element_type=F32)
    for e in range(2):
        out_ref[e] = part[e * rank : (e + 1) * rank]


def contrib_part(both, weight, index, parts):
    count, rows = both.shape
    cols = weight.shape[1] // parts
    tile = 512 if cols % 512 == 0 else cols
    steps = cols // tile
    return pl.pallas_call(
        contrib_kernel,
        grid=(steps,),
        out_shape=jax.ShapeDtypeStruct((2, count // 2, cols), F32),
        in_specs=[
            pl.BlockSpec((count, rows), lambda i: (0, 0)),
            pl.BlockSpec((rows, tile), lambda i: (0, index * steps + i)),
        ],
        out_specs=pl.BlockSpec((2, count // 2, tile), lambda i: (0, 0, i)),
        compiler_params=pltpu.CompilerParams(vmem_limit_bytes=VMEM_LIMIT),
        cost_estimate=pl.CostEstimate(
            flops=2 * count * rows * cols, bytes_accessed=2 * rows * cols, transcendentals=0
        ),
    )(both, weight)


def from_cycle(block, axis, distance):
    count = lax.axis_size(axis)
    return lax.ppermute(block, axis, [(i, (i + distance) % count) for i in range(count)])


def on_device(
    queries, keys, values, outputs, out_grad, log_norm, inputs, mlp_weight, initial_right_factor
):
    tok = queries.shape[1]
    heads = log_norm.shape[1]
    count = lax.axis_size("seq")
    me = lax.axis_index("seq")
    bits = gather_bits(count)
    factor = initial_right_factor[0]
    weight = mlp_weight[0]

    near = jnp.concatenate([keys[0], values[0]], axis=-1)
    packed = pack(inputs[0], count)
    acts_parts = []
    for index, bit in enumerate(bits):
        far = swap(near, "seq", bit, True if index == 0 else None)
        if index < PARTS:
            acts_parts.append(acts_part(factor, weight, index, PARTS))
        factor, near, far, packed, acts_parts = lax.optimization_barrier(
            (factor, near, far, packed, acts_parts)
        )
        if bit > 1:
            near = jnp.concatenate([near, far], axis=0)
    acts = jnp.concatenate(acts_parts, axis=1)

    feature_blocks = lax.all_to_all(packed, "seq", split_axis=0, concat_axis=0, tiled=True)
    lower_acts = from_cycle(acts, "rep", 1)
    higher_acts = from_cycle(acts, "rep", -1)

    delta = head_delta(out_grad[0], outputs[0], heads)
    query_grad, grads, sent = attend(me, queries[0], out_grad[0], log_norm[0], delta, near, far)
    lower_acts, higher_acts, sent = lax.optimization_barrier((lower_acts, higher_acts, sent))

    basis, both = make_basis(acts, lower_acts, higher_acts)
    contrib_parts = []
    for index, bit in enumerate(reversed(bits)):
        arrived = swap(sent, "seq", bit, False if bit == bits[0] else None)
        if index < PARTS:
            contrib_parts.append(contrib_part(both, weight, index, PARTS))
        both, grads, arrived, contrib_parts = lax.optimization_barrier(
            (both, grads, arrived, contrib_parts)
        )
        grads = grads + arrived.astype(F32)
        if bit < bits[0]:
            keep = grads.shape[0] // 2
            sent = grads[keep:].astype(BF16)
            grads = grads[:keep]
    contrib = jnp.concatenate(contrib_parts, axis=2)
    lower_half = from_cycle(contrib[1], "rep", 1)
    higher_half = from_cycle(contrib[0], "rep", -1)
    right_factor = jnp.stack([contrib[0] + lower_half, contrib[1] + higher_half], axis=0)

    near_b = grads.astype(BF16)
    for bit in bits:
        far_b = swap(near_b, "seq", bit)
        if bit > 1:
            near_b = jnp.concatenate([near_b, far_b], axis=0)
    proj_grad = project(me, feature_blocks, near_b, far_b)
    return (
        query_grad[None],
        grads[None],
        proj_grad[None],
        basis[None],
        right_factor[None, None],
    )


def solution(mesh):
    return jax.shard_map(
        on_device,
        mesh=mesh,
        in_specs=(
            P("rep", "seq", None),
            P("rep", "seq", None),
            P("rep", "seq", None),
            P("rep", "seq", None),
            P("rep", "seq", None),
            P("rep", None, "seq"),
            P("rep", "seq", None),
            P("rep", "seq", None),
            P("seq", None, None),
        ),
        out_specs=(
            P("rep", "seq", None),
            P("rep", "seq", None),
            P("rep", "seq", None),
            P("rep", None, None, "seq"),
            P("rep", "seq", None, None, None),
        ),
        check_vma=False,
    )
```

```python
import functools
import math

import jax
import jax.numpy as jnp
from jax import lax
from jax.experimental import pallas as pl
from jax.experimental.pallas import tpu as pltpu
from jax.sharding import PartitionSpec as P

WINDOW = 2048
EPSILON = 1e-06
LOG2E = math.log2(math.e)
F32 = jnp.float32
BF16 = jnp.bfloat16
VMEM_LIMIT = 48 * 1024 * 1024
PARTS = 3
STREAMS = 4
PARTS = 3
STREAMS = 4
COST = pl.CostEstimate(flops=1, bytes_accessed=1, transcendentals=0)


def dot_nt(a, b):
    return lax.dot_general(a, b, (((1,), (1,)), ((), ())), preferred_element_type=F32)


def dot_tn(a, b):
    return lax.dot_general(a, b, (((0,), (0,)), ((), ())), preferred_element_type=F32)


def vmem_specs(count):
    return [pl.BlockSpec(memory_space=pltpu.VMEM)] * count


def delta_kernel(head_dim, grad_ref, out_ref, delta_ref):
    for head in range(delta_ref.shape[0]):
        cols = slice(head * head_dim, (head + 1) * head_dim)
        prod = grad_ref[:, cols].astype(F32) * out_ref[:, cols].astype(F32)
        delta_ref[head : head + 1, :] = jnp.sum(prod.T, axis=0, keepdims=True)


def head_delta(out_grad, outputs, heads):
    rows, cols = out_grad.shape
    return pl.pallas_call(
        functools.partial(delta_kernel, cols // heads),
        out_shape=jax.ShapeDtypeStruct((heads, rows), F32),
        in_specs=vmem_specs(2),
        out_specs=pl.BlockSpec(memory_space=pltpu.VMEM),
        compiler_params=pltpu.CompilerParams(vmem_limit_bytes=VMEM_LIMIT),
        cost_estimate=COST,
    )(out_grad, outputs)


def swap(block, axis, bit, only_up=None):
    count = lax.axis_size(axis)
    route = [
        (i, i ^ bit) for i in range(count) if only_up is None or (i < i ^ bit) == only_up
    ]
    return lax.ppermute(block, axis, route)


def gather_bits(count):
    return [1 << b for b in reversed(range(count.bit_length() - 1))]


def gather_order(count):
    order = [0]
    for bit in gather_bits(count):
        order = order + [x ^ bit for x in order]
    return order


def swap(block, axis, bit, only_up=None):
    count = lax.axis_size(axis)
    route = [
        (i, i ^ bit) for i in range(count) if only_up is None or (i < i ^ bit) == only_up
    ]
    return lax.ppermute(block, axis, route)


def gather_bits(count):
    return [1 << b for b in reversed(range(count.bit_length() - 1))]


def gather_order(count):
    order = [0]
    for bit in gather_bits(count):
        order = order + [x ^ bit for x in order]
    return order


def attention_kernel(
    order, group, join, scale, me_ref, q_ref, do_ref, norm_ref, delta_ref, near_ref, far_ref,
    qg_ref, near_grad_ref, far_grad_ref, near_t_ref, far_t_ref, qgt_ref,
):
    tok = q_ref.shape[0]
    hd = near_ref.shape[1] // 2
    heads = norm_ref.shape[0]
    half = near_ref.shape[0]
    rows = join * tok
    me = me_ref[0]
    windowed = len(order) * tok > WINDOW
    chunks = [(s, first) for s in range(2) for first in range(0, half, rows)]
    kv_refs = (near_ref, far_ref)
    grad_refs = (near_grad_ref, far_grad_ref)
    t_refs = (near_t_ref, far_t_ref)
    for s, first in chunks:
        t_refs[s][:, first : first + rows] = kv_refs[s][first : first + rows, :hd].T
        grad_refs[s][first : first + rows, :] = jnp.zeros((rows, 2 * hd), F32)

    def step(index, carry):
        def stacked(ref):
            parts = []
            for i in range(group):
                first = pl.multiple_of((index * group + i) * hd, hd)
                parts.append(ref[:, pl.ds(first, hd)])
            return jnp.concatenate(parts, axis=0)

        def row(ref):
            return jnp.concatenate(
                [ref[pl.ds(index * group + i, 1), :] for i in range(group)], axis=1
            )

        q = stacked(q_ref)
        do = stacked(do_ref)
        norm = row(norm_ref) * LOG2E
        delta = row(delta_ref)
        qgt = None
        for s, first in chunks:
            area = slice(first, first + rows)
            key = kv_refs[s][area, :hd]
            value = kv_refs[s][area, hd:]
            logits = dot_nt(key, q) * (scale * LOG2E)
            parts = []
            for j in range(join):
                x = order[(s * half + first) // tok + j]
                source = me ^ x
                part = logits[j * tok : (j + 1) * tok]
                if x == 0 or windowed:
                    key_pos = source * tok + lax.broadcasted_iota(jnp.int32, part.shape, 0)
                    query = lax.broadcasted_iota(jnp.int32, part.shape, 1)
                    query_pos = me * tok + lax.rem(query, tok)
                    visible = (key_pos <= query_pos) & (key_pos > query_pos - WINDOW)
                    parts.append(jnp.where(visible, jnp.exp2(part - norm), 0.0))
                else:
                    hidden = jnp.where(source < me, 0.0, 1e30).astype(F32)
                    parts.append(jnp.exp2(part - (norm + hidden)))
            probs = jnp.concatenate(parts, axis=0)
            prob_grad = dot_nt(value, do)
            score_grad = (scale * probs * (prob_grad - delta)).astype(BF16)
            grad_refs[s][area, hd:] += jnp.dot(
                probs.astype(BF16), do, preferred_element_type=F32
            )
            grad_refs[s][area, :hd] += jnp.dot(score_grad, q, preferred_element_type=F32)
            part = jnp.dot(t_refs[s][:, area], score_grad, preferred_element_type=F32)
            qgt = part if qgt is None else qgt + part
        qgt_ref[...] = qgt
        for i in range(group):
            first = pl.multiple_of((index * group + i) * hd, hd)
            qg_ref[:, pl.ds(first, hd)] = qgt_ref[:, i * tok : (i + 1) * tok].T
        return carry

    lax.fori_loop(0, heads // group, step, 0)


def attend(me, queries, out_grad, norm, delta, near, far):
    tok, cols = queries.shape
    heads = norm.shape[0]
    hd = cols // heads
    half = near.shape[0]
    order = gather_order(2 * half // tok)
    group = next(g for g in (4, 3, 2, 1) if heads % g == 0)
    join = 2 if half % (2 * tok) == 0 else 1
    work = heads * tok * half * 2
    return pl.pallas_call(
        functools.partial(attention_kernel, order, group, join, hd ** (-0.5)),
        out_shape=[
            jax.ShapeDtypeStruct((tok, cols), F32),
            jax.ShapeDtypeStruct((half, 2 * hd), F32),
            jax.ShapeDtypeStruct((half, 2 * hd), F32),
        ],
        in_specs=[pl.BlockSpec(memory_space=pltpu.SMEM)] + vmem_specs(6),
        out_specs=vmem_specs(3),
        scratch_shapes=[
            pltpu.VMEM((hd, half), BF16),
            pltpu.VMEM((hd, half), BF16),
            pltpu.VMEM((hd, group * tok), F32),
        ],
        compiler_params=pltpu.CompilerParams(vmem_limit_bytes=VMEM_LIMIT),
        cost_estimate=pl.CostEstimate(
            flops=20 * work * hd, bytes_accessed=8 * tok * cols, transcendentals=work
        ),
    )(me[None], queries, out_grad, norm, delta, near, far)


def pack_kernel(width, me_ref, x_ref, *out_refs):
    me = me_ref[0]
    for x, out_ref in enumerate(out_refs):
        first = pl.multiple_of((me ^ x) * width, width)
        out_ref[...] = x_ref[:, pl.ds(first, width)]


def pack(me, inputs, count):
    tok, cols = inputs.shape
    width = cols // count
    if width % 128:
        return [
            lax.dynamic_slice_in_dim(inputs, (me ^ x) * width, width, axis=1)
            for x in range(count)
        ]
    return pl.pallas_call(
        functools.partial(pack_kernel, width),
        out_shape=[jax.ShapeDtypeStruct((tok, width), inputs.dtype)] * count,
        in_specs=[pl.BlockSpec(memory_space=pltpu.SMEM)] + vmem_specs(1),
        out_specs=vmem_specs(count),
        compiler_params=pltpu.CompilerParams(vmem_limit_bytes=VMEM_LIMIT),
        cost_estimate=pl.CostEstimate(
            flops=0, bytes_accessed=4 * tok * cols, transcendentals=0
        ),
    )(me[None], inputs)


def project_kernel(*refs):
    *x_refs, near_ref, far_ref, out_ref = refs
    x = jnp.concatenate([ref[...] for ref in x_refs], axis=0)
    grads = jnp.concatenate([near_ref[...], far_ref[...]], axis=0)
    out_ref[...] = dot_tn(x, grads)


def project(parts, near, far):
    tok, width = parts[0].shape
    cols = near.shape[1]
    return pl.pallas_call(
        project_kernel,
        out_shape=jax.ShapeDtypeStruct((width, cols), F32),
        in_specs=vmem_specs(len(parts) + 2),
        out_specs=pl.BlockSpec(memory_space=pltpu.VMEM),
        compiler_params=pltpu.CompilerParams(vmem_limit_bytes=VMEM_LIMIT),
        cost_estimate=pl.CostEstimate(
            flops=2 * len(parts) * tok * width * cols,
            bytes_accessed=2 * len(parts) * tok * width,
            transcendentals=0,
        ),
    )(*parts, near, far)


def acts_kernel(factor_ref, *refs):
    *w_refs, out_ref = refs
    rank, rows = out_ref.shape
    factor = factor_ref[...]
    parts = [dot_nt(ref[...], factor) for ref in w_refs]
    part = jnp.concatenate(parts, axis=0)
    wide = jnp.concatenate([part, jnp.zeros((rows, 128 - rank), F32)], axis=1)
    out_ref[...] = wide.T[:rank]


def acts_part(factor, weight, index, parts):
    rank, cols = factor.shape
    rows = weight.shape[0] // parts
    tile = 128 if rows % 128 == 0 else rows
    steps = rows // tile
    block = tile // STREAMS
    specs = [
        pl.BlockSpec((block, cols), lambda i, s=s: ((index * steps + i) * STREAMS + s, 0))
        for s in range(STREAMS)
    ]
    return pl.pallas_call(
        acts_kernel,
        grid=(steps,),
        out_shape=jax.ShapeDtypeStruct((rank, rows), F32),
        in_specs=[pl.BlockSpec((rank, cols), lambda i: (0, 0))] + specs,
        out_specs=pl.BlockSpec((rank, tile), lambda i: (0, i)),
        compiler_params=pltpu.CompilerParams(vmem_limit_bytes=VMEM_LIMIT),
        cost_estimate=pl.CostEstimate(
            flops=2 * rank * rows * cols, bytes_accessed=2 * rows * cols, transcendentals=0
        ),
    )(factor, *[weight] * STREAMS)


def orthonormal(diffs):
    columns = []
    for index in range(diffs.shape[0]):
        source = diffs[index : index + 1]
        vector = source
        for previous in columns:
            vector = vector - jnp.mean(source * previous, axis=-1, keepdims=True) * previous
        columns.append(
            vector * lax.rsqrt(jnp.mean(vector * vector, axis=-1, keepdims=True) + EPSILON)
        )
    return jnp.concatenate(columns, axis=0)


def basis_kernel(acts_ref, lower_ref, higher_ref, basis_ref, both_ref):
    acts = acts_ref[...]
    edges = [orthonormal(acts - ref[...]) for ref in (lower_ref, higher_ref)]
    for e, edge in enumerate(edges):
        basis_ref[e] = edge
    both_ref[...] = jnp.concatenate(edges, axis=0).astype(BF16)


def make_basis(acts, lower, higher):
    rank, rows = acts.shape
    return pl.pallas_call(
        basis_kernel,
        out_shape=[
            jax.ShapeDtypeStruct((2, rank, rows), F32),
            jax.ShapeDtypeStruct((2 * rank, rows), BF16),
        ],
        in_specs=vmem_specs(3),
        out_specs=vmem_specs(2),
        cost_estimate=pl.CostEstimate(
            flops=60 * rank * rows, bytes_accessed=40 * rank * rows, transcendentals=0
        ),
    )(acts, lower, higher)


def contrib_kernel(both_ref, *refs):
    *w_refs, out_ref = refs
    rank = out_ref.shape[1]
    block = w_refs[0].shape[0]
    part = None
    for s, ref in enumerate(w_refs):
        both = both_ref[:, s * block : (s + 1) * block]
        more = jnp.dot(both, ref[...], preferred_element_type=F32)
        part = more if part is None else part + more
    for e in range(2):
        out_ref[e] = part[e * rank : (e + 1) * rank]


def contrib_part(both, weight, index, parts):
    count, rows = both.shape
    cols = weight.shape[1] // parts
    tile = 512 if cols % 512 == 0 else cols
    steps = cols // tile
    block = rows // STREAMS
    specs = [
        pl.BlockSpec((block, tile), lambda i, s=s: (s, index * steps + i))
        for s in range(STREAMS)
    ]
    if block % 16:
        specs = [pl.BlockSpec((rows, tile), lambda i: (0, index * steps + i))]
    return pl.pallas_call(
        contrib_kernel,
        grid=(steps,),
        out_shape=jax.ShapeDtypeStruct((2, count // 2, cols), F32),
        in_specs=[pl.BlockSpec((count, rows), lambda i: (0, 0))] + specs,
        out_specs=pl.BlockSpec((2, count // 2, tile), lambda i: (0, 0, i)),
        compiler_params=pltpu.CompilerParams(vmem_limit_bytes=VMEM_LIMIT),
        cost_estimate=pl.CostEstimate(
            flops=2 * count * rows * cols, bytes_accessed=2 * rows * cols, transcendentals=0
        ),
    )(both, *[weight] * len(specs))


def from_cycle(block, axis, distance):
    count = lax.axis_size(axis)
    return lax.ppermute(block, axis, [(i, (i + distance) % count) for i in range(count)])


def on_device(
    queries, keys, values, outputs, out_grad, log_norm, inputs, mlp_weight, initial_right_factor
):
    tok = queries.shape[1]
    heads = log_norm.shape[1]
    count = lax.axis_size("seq")
    me = lax.axis_index("seq")
    bits = gather_bits(count)
    factor = initial_right_factor[0]
    weight = mlp_weight[0]

    far_parts = list(range(count // 2, count))
    near_parts = [x for x in range(1, count // 2) if x > 1] + ([1] if count > 2 else [])
    quarter = -(-len(far_parts) // 4)
    due = [far_parts[i * quarter : (i + 1) * quarter] for i in range(4)]
    packed = pack(me, inputs[0], count)
    parts = {0: packed[0]}

    def send(group):
        for x in group:
            parts[x] = swap(packed[x], "seq", x)

    def tie(group, values):
        values, held, rest = lax.optimization_barrier(
            (values, [parts[x] for x in group], [packed[x] for x in range(count)])
        )
        parts.update(zip(group, held))
        packed[:] = rest
        return values

    packed = list(packed)
    near = jnp.concatenate([keys[0], values[0]], axis=-1)
    near = tie([], near)

    acts_parts = []
    for index, bit in enumerate(bits):
        far = swap(near, "seq", bit, True if index == 0 else None)
        if index < 2:
            send(due[index])
        if index < PARTS:
            acts_parts.append(acts_part(factor, weight, index, PARTS))
        factor, near, far, acts_parts = tie(
            due[0] if index == 1 else [], (factor, near, far, acts_parts)
        )
        if bit > 1:
            near = jnp.concatenate([near, far], axis=0)
    acts = jnp.concatenate(acts_parts, axis=1)
    lower_acts = from_cycle(acts, "rep", 1)
    higher_acts = from_cycle(acts, "rep", -1)
    send(due[2])

    delta = head_delta(out_grad[0], outputs[0], heads)
    delta, near, far = tie(due[1], (delta, near, far))
    query_grad, grads, sent = attend(me, queries[0], out_grad[0], log_norm[0], delta, near, far)
    lower_acts, higher_acts, sent = tie(due[2], (lower_acts, higher_acts, sent))
    send(due[3])

    basis, both = make_basis(acts, lower_acts, higher_acts)
    contrib_parts = []
    for index, bit in enumerate(reversed(bits)):
        arrived = swap(sent, "seq", bit, False if bit == bits[0] else None)
        if index < PARTS:
            contrib_parts.append(contrib_part(both, weight, index, PARTS))
        if index == 1:
            send(near_parts)
        both, grads, arrived, contrib_parts = tie(
            due[3] if index == 1 else [],
            (both, grads, arrived, contrib_parts),
        )
        grads = grads + arrived.astype(F32)
        if bit < bits[0]:
            keep = grads.shape[0] // 2
            sent = grads[keep:].astype(BF16)
            grads = grads[:keep]
    contrib = jnp.concatenate(contrib_parts, axis=2)
    lower_half = from_cycle(contrib[1], "rep", 1)
    higher_half = from_cycle(contrib[0], "rep", -1)
    right_factor = jnp.stack([contrib[0] + lower_half, contrib[1] + higher_half], axis=0)

    near_b = grads.astype(BF16)
    for bit in bits:
        far_b = swap(near_b, "seq", bit)
        if bit > 1:
            near_b = jnp.concatenate([near_b, far_b], axis=0)
    proj_grad = project([parts[x] for x in gather_order(count)], near_b, far_b)
    return (
        query_grad[None],
        grads[None],
        proj_grad[None],
        basis[None],
        right_factor[None, None],
    )


def solution(mesh):
    return jax.shard_map(
        on_device,
        mesh=mesh,
        in_specs=(
            P("rep", "seq", None),
            P("rep", "seq", None),
            P("rep", "seq", None),
            P("rep", "seq", None),
            P("rep", "seq", None),
            P("rep", None, "seq"),
            P("rep", "seq", None),
            P("rep", "seq", None),
            P("seq", None, None),
        ),
        out_specs=(
            P("rep", "seq", None),
            P("rep", "seq", None),
            P("rep", "seq", None),
            P("rep", None, None, "seq"),
            P("rep", "seq", None, None, None),
        ),
        check_vma=False,
    )
```

```python
import functools
import math

import jax
import jax.numpy as jnp
from jax import lax
from jax.experimental import pallas as pl
from jax.experimental.pallas import tpu as pltpu
from jax.sharding import PartitionSpec as P

WINDOW = 2048
EPSILON = 1e-06
LOG2E = math.log2(math.e)
F32 = jnp.float32
BF16 = jnp.bfloat16
VMEM_LIMIT = 48 * 1024 * 1024
PARTS = 3
COST = pl.CostEstimate(flops=1, bytes_accessed=1, transcendentals=0)
PARTS = 3
COST = pl.CostEstimate(flops=1, bytes_accessed=1, transcendentals=0)
COST = pl.CostEstimate(flops=1, bytes_accessed=1, transcendentals=0)


def dot_nt(a, b):
    return lax.dot_general(a, b, (((1,), (1,)), ((), ())), preferred_element_type=F32)


def dot_tn(a, b):
    return lax.dot_general(a, b, (((0,), (0,)), ((), ())), preferred_element_type=F32)


def vmem_specs(count):
    return [pl.BlockSpec(memory_space=pltpu.VMEM)] * count


def delta_kernel(head_dim, grad_ref, out_ref, delta_ref):
    for head in range(delta_ref.shape[0]):
        cols = slice(head * head_dim, (head + 1) * head_dim)
        prod = grad_ref[:, cols].astype(F32) * out_ref[:, cols].astype(F32)
        delta_ref[head : head + 1, :] = jnp.sum(prod.T, axis=0, keepdims=True)


def head_delta(out_grad, outputs, heads):
    rows, cols = out_grad.shape
    return pl.pallas_call(
        functools.partial(delta_kernel, cols // heads),
        out_shape=jax.ShapeDtypeStruct((heads, rows), F32),
        in_specs=vmem_specs(2),
        out_specs=pl.BlockSpec(memory_space=pltpu.VMEM),
        compiler_params=pltpu.CompilerParams(vmem_limit_bytes=VMEM_LIMIT),
        cost_estimate=COST,
    )(out_grad, outputs)


def swap(block, axis, bit, only_up=None):
    count = lax.axis_size(axis)
    route = [
        (i, i ^ bit) for i in range(count) if only_up is None or (i < i ^ bit) == only_up
    ]
    return lax.ppermute(block, axis, route)


def gather_bits(count):
    return [1 << b for b in reversed(range(count.bit_length() - 1))]


def gather_order(count):
    order = [0]
    for bit in gather_bits(count):
        order = order + [x ^ bit for x in order]
    return order


def swap(block, axis, bit, only_up=None):
    count = lax.axis_size(axis)
    route = [
        (i, i ^ bit) for i in range(count) if only_up is None or (i < i ^ bit) == only_up
    ]
    return lax.ppermute(block, axis, route)


def gather_bits(count):
    return [1 << b for b in reversed(range(count.bit_length() - 1))]


def gather_order(count):
    order = [0]
    for bit in gather_bits(count):
        order = order + [x ^ bit for x in order]
    return order


def attention_kernel(
    order, group, join, scale, me_ref, q_ref, do_ref, norm_ref, delta_ref, near_ref, far_ref,
    qg_ref, near_grad_ref, far_grad_ref, near_t_ref, far_t_ref, qgt_ref,
):
    tok = q_ref.shape[0]
    hd = near_ref.shape[1] // 2
    heads = norm_ref.shape[0]
    half = near_ref.shape[0]
    rows = join * tok
    me = me_ref[0]
    windowed = len(order) * tok > WINDOW
    chunks = [(s, first) for s in range(2) for first in range(0, half, rows)]
    kv_refs = (near_ref, far_ref)
    grad_refs = (near_grad_ref, far_grad_ref)
    t_refs = (near_t_ref, far_t_ref)
    for s, first in chunks:
        t_refs[s][:, first : first + rows] = kv_refs[s][first : first + rows, :hd].T
        grad_refs[s][first : first + rows, :] = jnp.zeros((rows, 2 * hd), F32)

    def step(index, carry):
        def stacked(ref):
            parts = []
            for i in range(group):
                first = pl.multiple_of((index * group + i) * hd, hd)
                parts.append(ref[:, pl.ds(first, hd)])
            return jnp.concatenate(parts, axis=0)

        def row(ref):
            return jnp.concatenate(
                [ref[pl.ds(index * group + i, 1), :] for i in range(group)], axis=1
            )

        q = stacked(q_ref)
        do = stacked(do_ref)
        norm = row(norm_ref) * LOG2E
        delta = row(delta_ref)
        qgt = None
        for s, first in chunks:
            area = slice(first, first + rows)
            key = kv_refs[s][area, :hd]
            value = kv_refs[s][area, hd:]
            logits = dot_nt(key, q) * (scale * LOG2E)
            parts = []
            for j in range(join):
                x = order[(s * half + first) // tok + j]
                source = me ^ x
                part = logits[j * tok : (j + 1) * tok]
                if x == 0 or windowed:
                    key_pos = source * tok + lax.broadcasted_iota(jnp.int32, part.shape, 0)
                    query = lax.broadcasted_iota(jnp.int32, part.shape, 1)
                    query_pos = me * tok + lax.rem(query, tok)
                    visible = (key_pos <= query_pos) & (key_pos > query_pos - WINDOW)
                    parts.append(jnp.where(visible, jnp.exp2(part - norm), 0.0))
                else:
                    hidden = jnp.where(source < me, 0.0, 1e30).astype(F32)
                    parts.append(jnp.exp2(part - (norm + hidden)))
            probs = jnp.concatenate(parts, axis=0)
            prob_grad = dot_nt(value, do)
            score_grad = (scale * probs * (prob_grad - delta)).astype(BF16)
            grad_refs[s][area, hd:] += jnp.dot(
                probs.astype(BF16), do, preferred_element_type=F32
            )
            grad_refs[s][area, :hd] += jnp.dot(score_grad, q, preferred_element_type=F32)
            part = jnp.dot(t_refs[s][:, area], score_grad, preferred_element_type=F32)
            qgt = part if qgt is None else qgt + part
        qgt_ref[...] = qgt
        for i in range(group):
            first = pl.multiple_of((index * group + i) * hd, hd)
            qg_ref[:, pl.ds(first, hd)] = qgt_ref[:, i * tok : (i + 1) * tok].T
        return carry

    lax.fori_loop(0, heads // group, step, 0)


def attend(me, queries, out_grad, norm, delta, near, far):
    tok, cols = queries.shape
    heads = norm.shape[0]
    hd = cols // heads
    half = near.shape[0]
    order = gather_order(2 * half // tok)
    group = next(g for g in (4, 3, 2, 1) if heads % g == 0)
    join = 2 if half % (2 * tok) == 0 else 1
    return pl.pallas_call(
        functools.partial(attention_kernel, order, group, join, hd ** (-0.5)),
        out_shape=[
            jax.ShapeDtypeStruct((tok, cols), F32),
            jax.ShapeDtypeStruct((half, 2 * hd), F32),
            jax.ShapeDtypeStruct((half, 2 * hd), F32),
        ],
        in_specs=[pl.BlockSpec(memory_space=pltpu.SMEM)] + vmem_specs(6),
        out_specs=vmem_specs(3),
        scratch_shapes=[
            pltpu.VMEM((hd, half), BF16),
            pltpu.VMEM((hd, half), BF16),
            pltpu.VMEM((hd, group * tok), F32),
        ],
        compiler_params=pltpu.CompilerParams(vmem_limit_bytes=VMEM_LIMIT),
        cost_estimate=COST,
    )(me[None], queries, out_grad, norm, delta, near, far)


def pack_kernel(width, me_ref, x_ref, *out_refs):
    me = me_ref[0]
    for x, out_ref in enumerate(out_refs):
        first = pl.multiple_of((me ^ x) * width, width)
        out_ref[...] = x_ref[:, pl.ds(first, width)]


def pack(me, inputs, count):
    tok, cols = inputs.shape
    width = cols // count
    if width % 128:
        return [
            lax.dynamic_slice_in_dim(inputs, (me ^ x) * width, width, axis=1)
            for x in range(count)
        ]
    return pl.pallas_call(
        functools.partial(pack_kernel, width),
        out_shape=[jax.ShapeDtypeStruct((tok, width), inputs.dtype)] * count,
        in_specs=[pl.BlockSpec(memory_space=pltpu.SMEM)] + vmem_specs(1),
        out_specs=vmem_specs(count),
        compiler_params=pltpu.CompilerParams(vmem_limit_bytes=VMEM_LIMIT),
        cost_estimate=COST,
    )(me[None], inputs)


def project_kernel(*refs):
    *x_refs, near_ref, far_ref, out_ref = refs
    x = jnp.concatenate([ref[...] for ref in x_refs], axis=0)
    grads = jnp.concatenate([near_ref[...], far_ref[...]], axis=0)
    out_ref[...] = dot_tn(x, grads)


def project(parts, near, far):
    tok, width = parts[0].shape
    cols = near.shape[1]
    return pl.pallas_call(
        project_kernel,
        out_shape=jax.ShapeDtypeStruct((width, cols), F32),
        in_specs=vmem_specs(len(parts) + 2),
        out_specs=pl.BlockSpec(memory_space=pltpu.VMEM),
        compiler_params=pltpu.CompilerParams(vmem_limit_bytes=VMEM_LIMIT),
        cost_estimate=COST,
    )(*parts, near, far)


def acts_kernel(factor_ref, w_ref, out_ref, sum_ref):
    step = pl.program_id(0)
    rank, rows = out_ref.shape
    part = dot_nt(w_ref[...], factor_ref[...])

    @pl.when(step == 0)
    def _():
        sum_ref[...] = jnp.zeros_like(sum_ref)

    sum_ref[:, :rank] += part

    @pl.when(step == pl.num_programs(0) - 1)
    def _():
        out_ref[...] = sum_ref[...].T[:rank]


def acts_part(factor, weight, index, parts):
    rank, cols = factor.shape
    rows = weight.shape[0]
    tile = 512 if cols % (512 * parts) == 0 else cols // parts
    steps = cols // parts // tile
    return pl.pallas_call(
        acts_kernel,
        grid=(steps,),
        out_shape=jax.ShapeDtypeStruct((rank, rows), F32),
        in_specs=[
            pl.BlockSpec((rank, tile), lambda i: (0, index * steps + i)),
            pl.BlockSpec((rows, tile), lambda i: (0, index * steps + i)),
        ],
        out_specs=pl.BlockSpec((rank, rows), lambda i: (0, 0)),
        scratch_shapes=[pltpu.VMEM((rows, 128), F32)],
        compiler_params=pltpu.CompilerParams(vmem_limit_bytes=VMEM_LIMIT),
        cost_estimate=COST,
    )(factor, weight)


def orthonormal(rows):
    columns = []
    for source in rows:
        vector = source
        for previous in columns:
            vector = vector - jnp.mean(source * previous, axis=-1, keepdims=True) * previous
        columns.append(
            vector * lax.rsqrt(jnp.mean(vector * vector, axis=-1, keepdims=True) + EPSILON)
        )
    return columns


def basis_kernel(acts_ref, lower_ref, higher_ref, basis_ref, both_ref):
    rank = acts_ref.shape[0]
    rows = [
        acts_ref[k : k + 1]
        - jnp.concatenate([lower_ref[k : k + 1], higher_ref[k : k + 1]], axis=0)
        for k in range(rank)
    ]
    columns = orthonormal(rows)
    edges = [jnp.concatenate([c[e : e + 1] for c in columns], axis=0) for e in range(2)]
    for e, edge in enumerate(edges):
        basis_ref[e] = edge
    both_ref[...] = jnp.concatenate(edges, axis=0).astype(BF16)


def make_basis(acts, lower, higher):
    rank, rows = acts.shape
    return pl.pallas_call(
        basis_kernel,
        out_shape=[
            jax.ShapeDtypeStruct((2, rank, rows), F32),
            jax.ShapeDtypeStruct((2 * rank, rows), BF16),
        ],
        in_specs=vmem_specs(3),
        out_specs=vmem_specs(2),
        cost_estimate=COST,
    )(acts, lower, higher)


def contrib_kernel(both_ref, w_ref, out_ref):
    rank = out_ref.shape[1]
    part = jnp.dot(both_ref[...], w_ref[...], preferred_element_type=F32)
    for e in range(2):
        out_ref[e] = part[e * rank : (e + 1) * rank]


def contrib_part(both, weight, index, parts):
    count, rows = both.shape
    cols = weight.shape[1] // parts
    tile = 512 if cols % 512 == 0 else cols
    steps = cols // tile
    return pl.pallas_call(
        contrib_kernel,
        grid=(steps,),
        out_shape=jax.ShapeDtypeStruct((2, count // 2, cols), F32),
        in_specs=[
            pl.BlockSpec((count, rows), lambda i: (0, 0)),
            pl.BlockSpec((rows, tile), lambda i: (0, index * steps + i)),
        ],
        out_specs=pl.BlockSpec((2, count // 2, tile), lambda i: (0, 0, i)),
        compiler_params=pltpu.CompilerParams(vmem_limit_bytes=VMEM_LIMIT),
        cost_estimate=COST,
    )(both, weight)


def from_cycle(block, axis, distance):
    count = lax.axis_size(axis)
    return lax.ppermute(block, axis, [(i, (i + distance) % count) for i in range(count)])


def on_device(
    queries, keys, values, outputs, out_grad, log_norm, inputs, mlp_weight, initial_right_factor
):
    tok = queries.shape[1]
    heads = log_norm.shape[1]
    count = lax.axis_size("seq")
    me = lax.axis_index("seq")
    bits = gather_bits(count)
    factor = initial_right_factor[0]
    weight = mlp_weight[0]

    quarter = -(-(count // 2) // 4)
    due = [
        [x for x in range(count // 2 + i * quarter, count // 2 + (i + 1) * quarter) if x < count]
        for i in range(4)
    ]
    rest = list(range(2, count // 2)) + ([1] if count > 2 else [])
    packed = list(pack(me, inputs[0], count))
    parts = {0: packed[0]}

    def send(group):
        for x in group:
            parts[x] = swap(packed[x], "seq", x)

    def tie(group, values):
        values, held, packed[:] = lax.optimization_barrier(
            (values, [parts[x] for x in group], list(packed))
        )
        parts.update(zip(group, held))
        return values

    near = tie([], jnp.concatenate([keys[0], values[0]], axis=-1))
    acts = None
    for index, bit in enumerate(bits):
        far = swap(near, "seq", bit, True if index == 0 else None)
        if index < 2:
            send(due[index])
        if index < PARTS:
            part = acts_part(factor, weight, index, PARTS)
            acts = part if acts is None else acts + part
        factor, near, far, acts = tie(due[0] if index == 1 else [], (factor, near, far, acts))
        if bit > 1:
            near = jnp.concatenate([near, far], axis=0)
    lower_acts = from_cycle(acts, "rep", 1)
    higher_acts = from_cycle(acts, "rep", -1)
    send(due[2])

    delta = head_delta(out_grad[0], outputs[0], heads)
    delta, near, far = tie(due[1], (delta, near, far))
    query_grad, grads, sent = attend(me, queries[0], out_grad[0], log_norm[0], delta, near, far)
    lower_acts, higher_acts, sent = tie(due[2], (lower_acts, higher_acts, sent))
    send(due[3])

    basis, both = make_basis(acts, lower_acts, higher_acts)
    contrib_parts = []
    last = bits[0]
    for index, bit in enumerate(b for b in reversed(bits) if b != last):
        arrived = swap(sent, "seq", bit)
        share = PARTS - index if bit * 2 == last else 1
        if index < PARTS:
            contrib_parts += [
                contrib_part(both, weight, index + i, PARTS) for i in range(share)
            ]
        if bit * 2 == last:
            send(rest)
        both, grads, arrived, contrib_parts = tie(
            due[3] if bit * 2 == last else [], (both, grads, arrived, contrib_parts)
        )
        grads = grads + arrived.astype(F32)
        keep = grads.shape[0] // 2
        if bit * 2 < last:
            sent = grads[keep:].astype(BF16)
            grads = grads[:keep]
    contrib = jnp.concatenate(contrib_parts, axis=2)
    lower_half = from_cycle(contrib[1], "rep", 1)
    higher_half = from_cycle(contrib[0], "rep", -1)

    upper = (me & last) != 0
    arrived = swap(grads.astype(BF16), "seq", last).astype(F32)
    mine, theirs = grads[:keep], grads[keep:]
    own = jnp.where(upper, mine, mine + arrived[keep:])
    other = jnp.where(upper, theirs + arrived[:keep], arrived[:keep])
    near_b = jnp.concatenate([own, other], axis=0).astype(BF16)
    for bit in bits[1:]:
        far_b = swap(near_b, "seq", bit)
        if bit > 1:
            near_b = jnp.concatenate([near_b, far_b], axis=0)
    proj_grad = project([parts[x] for x in gather_order(count)], near_b, far_b)
    right_factor = jnp.stack([contrib[0] + lower_half, contrib[1] + higher_half], axis=0)
    return (
        query_grad[None],
        own[None],
        proj_grad[None],
        basis[None],
        right_factor[None, None],
    )


def solution(mesh):
    return jax.shard_map(
        on_device,
        mesh=mesh,
        in_specs=(
            P("rep", "seq", None),
            P("rep", "seq", None),
            P("rep", "seq", None),
            P("rep", "seq", None),
            P("rep", "seq", None),
            P("rep", None, "seq"),
            P("rep", "seq", None),
            P("rep", "seq", None),
            P("seq", None, None),
        ),
        out_specs=(
            P("rep", "seq", None),
            P("rep", "seq", None),
            P("rep", "seq", None),
            P("rep", None, None, "seq"),
            P("rep", "seq", None, None, None),
        ),
        check_vma=False,
    )
```

```python
import functools
import math

import jax
import jax.numpy as jnp
from jax import lax
from jax.experimental import pallas as pl
from jax.experimental.pallas import tpu as pltpu
from jax.sharding import PartitionSpec as P

WINDOW = 2048
EPSILON = 1e-06
LOG2E = math.log2(math.e)
F32 = jnp.float32
BF16 = jnp.bfloat16
VMEM_LIMIT = 48 * 1024 * 1024
PARTS = 2
COST = pl.CostEstimate(flops=1, bytes_accessed=1, transcendentals=0)
PARTS = 2
COST = pl.CostEstimate(flops=1, bytes_accessed=1, transcendentals=0)
COST = pl.CostEstimate(flops=1, bytes_accessed=1, transcendentals=0)


def dot_nt(a, b):
    return lax.dot_general(a, b, (((1,), (1,)), ((), ())), preferred_element_type=F32)


def dot_tn(a, b):
    return lax.dot_general(a, b, (((0,), (0,)), ((), ())), preferred_element_type=F32)


def vmem_specs(count):
    return [pl.BlockSpec(memory_space=pltpu.VMEM)] * count


def delta_kernel(head_dim, grad_ref, out_ref, delta_ref):
    for head in range(delta_ref.shape[0]):
        cols = slice(head * head_dim, (head + 1) * head_dim)
        prod = grad_ref[:, cols].astype(F32) * out_ref[:, cols].astype(F32)
        delta_ref[head : head + 1, :] = jnp.sum(prod.T, axis=0, keepdims=True)


def head_delta(out_grad, outputs, heads):
    rows, cols = out_grad.shape
    return pl.pallas_call(
        functools.partial(delta_kernel, cols // heads),
        out_shape=jax.ShapeDtypeStruct((heads, rows), F32),
        in_specs=vmem_specs(2),
        out_specs=pl.BlockSpec(memory_space=pltpu.VMEM),
        compiler_params=pltpu.CompilerParams(vmem_limit_bytes=VMEM_LIMIT),
        cost_estimate=COST,
    )(out_grad, outputs)


def swap(block, axis, bit, only_up=None):
    count = lax.axis_size(axis)
    route = [
        (i, i ^ bit) for i in range(count) if only_up is None or (i < i ^ bit) == only_up
    ]
    return lax.ppermute(block, axis, route)


def gather_bits(count):
    return [1 << b for b in reversed(range(count.bit_length() - 1))]


def gather_order(count):
    order = [0]
    for bit in gather_bits(count):
        order = order + [x ^ bit for x in order]
    return order


def swap(block, axis, bit, only_up=None):
    count = lax.axis_size(axis)
    route = [
        (i, i ^ bit) for i in range(count) if only_up is None or (i < i ^ bit) == only_up
    ]
    return lax.ppermute(block, axis, route)


def gather_bits(count):
    return [1 << b for b in reversed(range(count.bit_length() - 1))]


def gather_order(count):
    order = [0]
    for bit in gather_bits(count):
        order = order + [x ^ bit for x in order]
    return order


def attention_kernel(
    order, group, join, scale, me_ref, q_ref, do_ref, norm_ref, delta_ref, near_ref, far_ref,
    qg_ref, near_grad_ref, far_grad_ref, near_t_ref, far_t_ref, qgt_ref,
):
    tok = q_ref.shape[0]
    hd = near_ref.shape[1] // 2
    heads = norm_ref.shape[0]
    half = near_ref.shape[0]
    rows = join * tok
    me = me_ref[0]
    windowed = len(order) * tok > WINDOW
    chunks = [(s, first) for s in range(2) for first in range(0, half, rows)]
    kv_refs = (near_ref, far_ref)
    grad_refs = (near_grad_ref, far_grad_ref)
    t_refs = (near_t_ref, far_t_ref)
    for s, first in chunks:
        t_refs[s][:, first : first + rows] = kv_refs[s][first : first + rows, :hd].T
        grad_refs[s][first : first + rows, :] = jnp.zeros((rows, 2 * hd), F32)

    def step(index, carry):
        def stacked(ref):
            parts = []
            for i in range(group):
                first = pl.multiple_of((index * group + i) * hd, hd)
                parts.append(ref[:, pl.ds(first, hd)])
            return jnp.concatenate(parts, axis=0)

        def row(ref):
            return jnp.concatenate(
                [ref[pl.ds(index * group + i, 1), :] for i in range(group)], axis=1
            )

        q = stacked(q_ref)
        do = stacked(do_ref)
        norm = row(norm_ref) * LOG2E
        delta = row(delta_ref)
        qgt = None
        for s, first in chunks:
            area = slice(first, first + rows)
            key = kv_refs[s][area, :hd]
            value = kv_refs[s][area, hd:]
            logits = dot_nt(key, q) * (scale * LOG2E)
            parts = []
            for j in range(join):
                x = order[(s * half + first) // tok + j]
                source = me ^ x
                part = logits[j * tok : (j + 1) * tok]
                if x == 0 or windowed:
                    key_pos = source * tok + lax.broadcasted_iota(jnp.int32, part.shape, 0)
                    query = lax.broadcasted_iota(jnp.int32, part.shape, 1)
                    query_pos = me * tok + lax.rem(query, tok)
                    visible = (key_pos <= query_pos) & (key_pos > query_pos - WINDOW)
                    parts.append(jnp.where(visible, jnp.exp2(part - norm), 0.0))
                else:
                    hidden = jnp.where(source < me, 0.0, 1e30).astype(F32)
                    parts.append(jnp.exp2(part - (norm + hidden)))
            probs = jnp.concatenate(parts, axis=0)
            prob_grad = dot_nt(value, do)
            score_grad = (scale * probs * (prob_grad - delta)).astype(BF16)
            grad_refs[s][area, hd:] += jnp.dot(
                probs.astype(BF16), do, preferred_element_type=F32
            )
            grad_refs[s][area, :hd] += jnp.dot(score_grad, q, preferred_element_type=F32)
            part = jnp.dot(t_refs[s][:, area], score_grad, preferred_element_type=F32)
            qgt = part if qgt is None else qgt + part
        qgt_ref[...] = qgt
        for i in range(group):
            first = pl.multiple_of((index * group + i) * hd, hd)
            qg_ref[:, pl.ds(first, hd)] = qgt_ref[:, i * tok : (i + 1) * tok].T
        return carry

    lax.fori_loop(0, heads // group, step, 0)


def attend(me, queries, out_grad, norm, delta, near, far):
    tok, cols = queries.shape
    heads = norm.shape[0]
    hd = cols // heads
    half = near.shape[0]
    order = gather_order(2 * half // tok)
    group = next(g for g in (4, 3, 2, 1) if heads % g == 0)
    join = 2 if half % (2 * tok) == 0 else 1
    return pl.pallas_call(
        functools.partial(attention_kernel, order, group, join, hd ** (-0.5)),
        out_shape=[
            jax.ShapeDtypeStruct((tok, cols), F32),
            jax.ShapeDtypeStruct((half, 2 * hd), F32),
            jax.ShapeDtypeStruct((half, 2 * hd), F32),
        ],
        in_specs=[pl.BlockSpec(memory_space=pltpu.SMEM)] + vmem_specs(6),
        out_specs=vmem_specs(3),
        scratch_shapes=[
            pltpu.VMEM((hd, half), BF16),
            pltpu.VMEM((hd, half), BF16),
            pltpu.VMEM((hd, group * tok), F32),
        ],
        compiler_params=pltpu.CompilerParams(vmem_limit_bytes=VMEM_LIMIT),
        cost_estimate=COST,
    )(me[None], queries, out_grad, norm, delta, near, far)


def pack_kernel(x_ref, out_ref):
    width = out_ref.shape[2]
    for j in range(out_ref.shape[0]):
        out_ref[j] = x_ref[:, j * width : (j + 1) * width]


def pack(inputs, chips):
    tok, cols = inputs.shape
    return pl.pallas_call(
        pack_kernel,
        out_shape=jax.ShapeDtypeStruct((chips, tok, cols // chips), inputs.dtype),
        in_specs=vmem_specs(1),
        out_specs=pl.BlockSpec(memory_space=pltpu.VMEM),
        compiler_params=pltpu.CompilerParams(vmem_limit_bytes=VMEM_LIMIT),
        cost_estimate=COST,
    )(inputs)


def project_kernel(order, me_ref, x_ref, grads_ref, mine_ref, theirs_ref):
    chip = me_ref[0] // 2
    x = jnp.concatenate([x_ref[chip ^ part] for part in order], axis=0)
    width = mine_ref.shape[0]
    grads = grads_ref[...]
    odd = lax.rem(me_ref[0], 2) == 1
    first = dot_tn(x[:, :width], grads)
    second = dot_tn(x[:, width:], grads)
    mine_ref[...] = jnp.where(odd, second, first)
    theirs_ref[...] = jnp.where(odd, first, second)


def project(me, blocks, grads, order):
    width = blocks.shape[2] // 2
    return pl.pallas_call(
        functools.partial(project_kernel, order),
        out_shape=[jax.ShapeDtypeStruct((width, grads.shape[1]), F32)] * 2,
        in_specs=[pl.BlockSpec(memory_space=pltpu.SMEM)] + vmem_specs(2),
        out_specs=vmem_specs(2),
        compiler_params=pltpu.CompilerParams(vmem_limit_bytes=VMEM_LIMIT),
        cost_estimate=COST,
    )(me[None], blocks, grads)


def acts_part(factor, weight, index, parts):
    rows = weight.shape[0] // parts
    some = weight[index * rows : (index + 1) * rows]
    return dot_nt(factor, some)


def contrib_part(both, weight, index, parts):
    cols = weight.shape[1] // parts
    some = weight[:, index * cols : (index + 1) * cols]
    part = jnp.dot(both, some, preferred_element_type=F32)
    return part.reshape(2, both.shape[0] // 2, cols)


def orthonormal(rows):
    columns = []
    for source in rows:
        vector = source
        for previous in columns:
            vector = vector - jnp.mean(source * previous, axis=-1, keepdims=True) * previous
        columns.append(
            vector * lax.rsqrt(jnp.mean(vector * vector, axis=-1, keepdims=True) + EPSILON)
        )
    return columns


def basis_kernel(acts_ref, lower_ref, higher_ref, basis_ref, both_ref):
    rank = acts_ref.shape[0]
    rows = [
        acts_ref[k : k + 1]
        - jnp.concatenate([lower_ref[k : k + 1], higher_ref[k : k + 1]], axis=0)
        for k in range(rank)
    ]
    columns = orthonormal(rows)
    edges = [jnp.concatenate([c[e : e + 1] for c in columns], axis=0) for e in range(2)]
    for e, edge in enumerate(edges):
        basis_ref[e] = edge
    both_ref[...] = jnp.concatenate(edges, axis=0).astype(BF16)


def make_basis(acts, lower, higher):
    rank, rows = acts.shape
    return pl.pallas_call(
        basis_kernel,
        out_shape=[
            jax.ShapeDtypeStruct((2, rank, rows), F32),
            jax.ShapeDtypeStruct((2 * rank, rows), BF16),
        ],
        in_specs=vmem_specs(3),
        out_specs=vmem_specs(2),
        cost_estimate=COST,
    )(acts, lower, higher)


def from_cycle(block, axis, distance):
    count = lax.axis_size(axis)
    return lax.ppermute(block, axis, [(i, (i + distance) % count) for i in range(count)])


def on_device(
    queries, keys, values, outputs, out_grad, log_norm, inputs, mlp_weight, initial_right_factor
):
    tok = queries.shape[1]
    heads = log_norm.shape[1]
    count = lax.axis_size("seq")
    me = lax.axis_index("seq")
    bits = gather_bits(count)
    factor = initial_right_factor[0]
    weight = mlp_weight[0]

    chips = count // 2
    packed = pack(inputs[0], chips)
    near = jnp.concatenate([keys[0], values[0]], axis=-1)
    near, packed = lax.optimization_barrier((near, packed))
    blocks = lax.all_to_all(
        packed,
        "seq",
        split_axis=0,
        concat_axis=0,
        tiled=True,
        axis_index_groups=[list(range(core, count, 2)) for core in range(2)],
    )

    acts_parts = []
    for index, bit in enumerate(bits):
        far = swap(near, "seq", bit, True if index == 0 else None)
        if index < PARTS:
            acts_parts.append(acts_part(factor, weight, index, PARTS))
        factor, near, far, acts_parts = lax.optimization_barrier(
            (factor, near, far, acts_parts)
        )
        if bit > 1:
            near = jnp.concatenate([near, far], axis=0)
    acts = jnp.concatenate(acts_parts, axis=1)
    lower_acts = from_cycle(acts, "rep", 1)
    higher_acts = from_cycle(acts, "rep", -1)

    delta = head_delta(out_grad[0], outputs[0], heads)
    delta, near, far = lax.optimization_barrier((delta, near, far))
    query_grad, grads, sent = attend(me, queries[0], out_grad[0], log_norm[0], delta, near, far)
    lower_acts, higher_acts, sent = lax.optimization_barrier((lower_acts, higher_acts, sent))

    basis, both = make_basis(acts, lower_acts, higher_acts)
    contrib_parts = []
    last = bits[0]
    for index, bit in enumerate(b for b in reversed(bits) if b != last):
        arrived = swap(sent, "seq", bit)
        share = PARTS - index if bit * 2 == last else 1
        if index < PARTS:
            contrib_parts += [
                contrib_part(both, weight, index + i, PARTS) for i in range(share)
            ]
        both, grads, arrived, contrib_parts, blocks = lax.optimization_barrier(
            (both, grads, arrived, contrib_parts, blocks)
        ) if bit * 2 == last else (
            *lax.optimization_barrier((both, grads, arrived, contrib_parts)), blocks
        )
        grads = grads + arrived.astype(F32)
        keep = grads.shape[0] // 2
        if bit * 2 < last:
            sent = grads[keep:].astype(BF16)
            grads = grads[:keep]
    contrib = jnp.concatenate(contrib_parts, axis=2)
    lower_half = from_cycle(contrib[1], "rep", 1)
    higher_half = from_cycle(contrib[0], "rep", -1)

    upper = (me & last) != 0
    arrived = swap(grads.astype(BF16), "seq", last).astype(F32)
    mine, theirs = grads[:keep], grads[keep:]
    own = jnp.where(upper, mine, mine + arrived[keep:])
    other = jnp.where(upper, theirs + arrived[:keep], arrived[:keep])
    near_b = jnp.concatenate([own, other], axis=0).astype(BF16)
    for bit in bits[1:-1]:
        near_b = jnp.concatenate([near_b, swap(near_b, "seq", bit)], axis=0)
    order = [x // 2 for x in gather_order(count)[: count // 2]]
    proj_mine, proj_theirs = project(me, blocks, near_b, order)
    proj_grad = proj_mine + swap(proj_theirs, "seq", 1)
    right_factor = jnp.stack([contrib[0] + lower_half, contrib[1] + higher_half], axis=0)
    return (
        query_grad[None],
        own[None],
        proj_grad[None],
        basis[None],
        right_factor[None, None],
    )


def solution(mesh):
    return jax.shard_map(
        on_device,
        mesh=mesh,
        in_specs=(
            P("rep", "seq", None),
            P("rep", "seq", None),
            P("rep", "seq", None),
            P("rep", "seq", None),
            P("rep", "seq", None),
            P("rep", None, "seq"),
            P("rep", "seq", None),
            P("rep", "seq", None),
            P("seq", None, None),
        ),
        out_specs=(
            P("rep", "seq", None),
            P("rep", "seq", None),
            P("rep", "seq", None),
            P("rep", None, None, "seq"),
            P("rep", "seq", None, None, None),
        ),
        check_vma=False,
    )
```

```python
import functools
import math

import jax
import jax.numpy as jnp
from jax import lax
from jax.experimental import pallas as pl
from jax.experimental.pallas import tpu as pltpu
from jax.sharding import PartitionSpec as P

WINDOW = 2048
EPSILON = 1e-06
LOG2E = math.log2(math.e)
F32 = jnp.float32
BF16 = jnp.bfloat16
VMEM_LIMIT = 48 * 1024 * 1024
PARTS = 2
COST = pl.CostEstimate(flops=1, bytes_accessed=1, transcendentals=0)
PARTS = 2
COST = pl.CostEstimate(flops=1, bytes_accessed=1, transcendentals=0)
COST = pl.CostEstimate(flops=1, bytes_accessed=1, transcendentals=0)


def dot_nt(a, b):
    return lax.dot_general(a, b, (((1,), (1,)), ((), ())), preferred_element_type=F32)


def dot_tn(a, b):
    return lax.dot_general(a, b, (((0,), (0,)), ((), ())), preferred_element_type=F32)


def vmem_specs(count):
    return [pl.BlockSpec(memory_space=pltpu.VMEM)] * count


def delta_kernel(head_dim, grad_ref, out_ref, delta_ref):
    for head in range(delta_ref.shape[0]):
        cols = slice(head * head_dim, (head + 1) * head_dim)
        prod = grad_ref[:, cols].astype(F32) * out_ref[:, cols].astype(F32)
        delta_ref[head : head + 1, :] = jnp.sum(prod.T, axis=0, keepdims=True)


def head_delta(out_grad, outputs, heads):
    rows, cols = out_grad.shape
    return pl.pallas_call(
        functools.partial(delta_kernel, cols // heads),
        out_shape=jax.ShapeDtypeStruct((heads, rows), F32),
        in_specs=vmem_specs(2),
        out_specs=pl.BlockSpec(memory_space=pltpu.VMEM),
        compiler_params=pltpu.CompilerParams(vmem_limit_bytes=VMEM_LIMIT),
        cost_estimate=COST,
    )(out_grad, outputs)


def swap(block, axis, bit, only_up=None):
    count = lax.axis_size(axis)
    route = [
        (i, i ^ bit) for i in range(count) if only_up is None or (i < i ^ bit) == only_up
    ]
    return lax.ppermute(block, axis, route)


def gather_bits(count):
    return [1 << b for b in reversed(range(count.bit_length() - 1))]


def gather_order(count):
    order = [0]
    for bit in gather_bits(count):
        order = order + [x ^ bit for x in order]
    return order


def swap(block, axis, bit, only_up=None):
    count = lax.axis_size(axis)
    route = [
        (i, i ^ bit) for i in range(count) if only_up is None or (i < i ^ bit) == only_up
    ]
    return lax.ppermute(block, axis, route)


def gather_bits(count):
    return [1 << b for b in reversed(range(count.bit_length() - 1))]


def gather_order(count):
    order = [0]
    for bit in gather_bits(count):
        order = order + [x ^ bit for x in order]
    return order


def attention_kernel(
    order, group, join, scale, me_ref, q_ref, do_ref, norm_ref, delta_ref, near_ref, far_ref,
    qg_ref, near_grad_ref, far_grad_ref, near_t_ref, far_t_ref, qgt_ref,
):
    tok = q_ref.shape[0]
    hd = near_ref.shape[1] // 2
    heads = norm_ref.shape[0]
    half = near_ref.shape[0]
    rows = join * tok
    me = me_ref[0]
    windowed = len(order) * tok > WINDOW
    chunks = [(s, first) for s in range(2) for first in range(0, half, rows)]
    kv_refs = (near_ref, far_ref)
    grad_refs = (near_grad_ref, far_grad_ref)
    t_refs = (near_t_ref, far_t_ref)
    for s, first in chunks:
        t_refs[s][:, first : first + rows] = kv_refs[s][first : first + rows, :hd].T
        grad_refs[s][first : first + rows, :] = jnp.zeros((rows, 2 * hd), F32)

    def step(index, carry):
        def stacked(ref):
            parts = []
            for i in range(group):
                first = pl.multiple_of((index * group + i) * hd, hd)
                parts.append(ref[:, pl.ds(first, hd)])
            return jnp.concatenate(parts, axis=0)

        def row(ref):
            return jnp.concatenate(
                [ref[pl.ds(index * group + i, 1), :] for i in range(group)], axis=1
            )

        q = stacked(q_ref)
        do = stacked(do_ref)
        norm = row(norm_ref) * LOG2E
        delta = row(delta_ref)
        qgt = None
        for s, first in chunks:
            area = slice(first, first + rows)
            key = kv_refs[s][area, :hd]
            value = kv_refs[s][area, hd:]
            logits = dot_nt(key, q) * (scale * LOG2E)
            parts = []
            for j in range(join):
                x = order[(s * half + first) // tok + j]
                source = me ^ x
                part = logits[j * tok : (j + 1) * tok]
                if x == 0 or windowed:
                    key_pos = source * tok + lax.broadcasted_iota(jnp.int32, part.shape, 0)
                    query = lax.broadcasted_iota(jnp.int32, part.shape, 1)
                    query_pos = me * tok + lax.rem(query, tok)
                    visible = (key_pos <= query_pos) & (key_pos > query_pos - WINDOW)
                    parts.append(jnp.where(visible, jnp.exp2(part - norm), 0.0))
                else:
                    hidden = jnp.where(source < me, 0.0, 1e30).astype(F32)
                    parts.append(jnp.exp2(part - (norm + hidden)))
            probs = jnp.concatenate(parts, axis=0)
            prob_grad = dot_nt(value, do)
            score_grad = (scale * probs * (prob_grad - delta)).astype(BF16)
            grad_refs[s][area, hd:] += jnp.dot(
                probs.astype(BF16), do, preferred_element_type=F32
            )
            grad_refs[s][area, :hd] += jnp.dot(score_grad, q, preferred_element_type=F32)
            part = jnp.dot(t_refs[s][:, area], score_grad, preferred_element_type=F32)
            qgt = part if qgt is None else qgt + part
        qgt_ref[...] = qgt
        for i in range(group):
            first = pl.multiple_of((index * group + i) * hd, hd)
            qg_ref[:, pl.ds(first, hd)] = qgt_ref[:, i * tok : (i + 1) * tok].T
        return carry

    lax.fori_loop(0, heads // group, step, 0)


def attend(me, queries, out_grad, norm, delta, near, far):
    tok, cols = queries.shape
    heads = norm.shape[0]
    hd = cols // heads
    half = near.shape[0]
    order = gather_order(2 * half // tok)
    group = next(g for g in (4, 3, 2, 1) if heads % g == 0)
    join = 2 if half % (2 * tok) == 0 else 1
    return pl.pallas_call(
        functools.partial(attention_kernel, order, group, join, hd ** (-0.5)),
        out_shape=[
            jax.ShapeDtypeStruct((tok, cols), F32),
            jax.ShapeDtypeStruct((half, 2 * hd), F32),
            jax.ShapeDtypeStruct((half, 2 * hd), F32),
        ],
        in_specs=[pl.BlockSpec(memory_space=pltpu.SMEM)] + vmem_specs(6),
        out_specs=vmem_specs(3),
        scratch_shapes=[
            pltpu.VMEM((hd, half), BF16),
            pltpu.VMEM((hd, half), BF16),
            pltpu.VMEM((hd, group * tok), F32),
        ],
        compiler_params=pltpu.CompilerParams(vmem_limit_bytes=VMEM_LIMIT),
        cost_estimate=COST,
    )(me[None], queries, out_grad, norm, delta, near, far)


def pack_kernel(x_ref, out_ref):
    width = out_ref.shape[2]
    for j in range(out_ref.shape[0]):
        out_ref[j] = x_ref[:, j * width : (j + 1) * width]


def pack(inputs, chips):
    tok, cols = inputs.shape
    return pl.pallas_call(
        pack_kernel,
        out_shape=jax.ShapeDtypeStruct((chips, tok, cols // chips), inputs.dtype),
        in_specs=vmem_specs(1),
        out_specs=pl.BlockSpec(memory_space=pltpu.VMEM),
        compiler_params=pltpu.CompilerParams(vmem_limit_bytes=VMEM_LIMIT),
        cost_estimate=COST,
    )(inputs)


def project_kernel(order, me_ref, x_ref, grads_ref, mine_ref, theirs_ref):
    chip = me_ref[0] // 2
    x = jnp.concatenate([x_ref[chip ^ part] for part in order], axis=0)
    width = mine_ref.shape[0]
    grads = grads_ref[...]
    odd = lax.rem(me_ref[0], 2) == 1
    first = dot_tn(x[:, :width], grads)
    second = dot_tn(x[:, width:], grads)
    mine_ref[...] = jnp.where(odd, second, first)
    theirs_ref[...] = jnp.where(odd, first, second)


def project(me, blocks, grads, order):
    width = blocks.shape[2] // 2
    return pl.pallas_call(
        functools.partial(project_kernel, order),
        out_shape=[jax.ShapeDtypeStruct((width, grads.shape[1]), F32)] * 2,
        in_specs=[pl.BlockSpec(memory_space=pltpu.SMEM)] + vmem_specs(2),
        out_specs=vmem_specs(2),
        compiler_params=pltpu.CompilerParams(vmem_limit_bytes=VMEM_LIMIT),
        cost_estimate=COST,
    )(me[None], blocks, grads)


def contrib_part(both, weight, index, parts):
    cols = weight.shape[1] // parts
    some = weight[:, index * cols : (index + 1) * cols]
    part = jnp.dot(both, some, preferred_element_type=F32)
    return part.reshape(2, both.shape[0] // 2, cols)


def orthonormal(rows):
    columns = []
    for source in rows:
        vector = source
        for previous in columns:
            vector = vector - jnp.mean(source * previous, axis=-1, keepdims=True) * previous
        columns.append(
            vector * lax.rsqrt(jnp.mean(vector * vector, axis=-1, keepdims=True) + EPSILON)
        )
    return columns


def basis_kernel(acts_ref, lower_ref, higher_ref, basis_ref, both_ref):
    rank = acts_ref.shape[0]
    rows = [
        acts_ref[k : k + 1]
        - jnp.concatenate([lower_ref[k : k + 1], higher_ref[k : k + 1]], axis=0)
        for k in range(rank)
    ]
    columns = orthonormal(rows)
    edges = [jnp.concatenate([c[e : e + 1] for c in columns], axis=0) for e in range(2)]
    for e, edge in enumerate(edges):
        basis_ref[e] = edge
    both_ref[...] = jnp.concatenate(edges, axis=0).astype(BF16)


def make_basis(acts, lower, higher):
    rank, rows = acts.shape
    return pl.pallas_call(
        basis_kernel,
        out_shape=[
            jax.ShapeDtypeStruct((2, rank, rows), F32),
            jax.ShapeDtypeStruct((2 * rank, rows), BF16),
        ],
        in_specs=vmem_specs(3),
        out_specs=vmem_specs(2),
        cost_estimate=COST,
    )(acts, lower, higher)


def from_cycle(block, axis, distance):
    count = lax.axis_size(axis)
    return lax.ppermute(block, axis, [(i, (i + distance) % count) for i in range(count)])


def on_device(
    queries, keys, values, outputs, out_grad, log_norm, inputs, mlp_weight, initial_right_factor
):
    tok = queries.shape[1]
    heads = log_norm.shape[1]
    count = lax.axis_size("seq")
    me = lax.axis_index("seq")
    bits = gather_bits(count)
    factor = initial_right_factor[0]
    weight = mlp_weight[0]

    near = jnp.concatenate([keys[0], values[0]], axis=-1)
    chips = count // 2
    beside = [pack(inputs[0], chips), head_delta(out_grad[0], outputs[0], heads), factor]
    for index, bit in enumerate(bits):
        if bit == 1:
            break
        far = swap(near, "seq", bit, True if index == 0 else None)
        near, far, beside = lax.optimization_barrier((near, far, beside))
        near = jnp.concatenate([near, far], axis=0)
    packed, delta, factor = beside
    blocks = lax.all_to_all(
        packed,
        "seq",
        split_axis=0,
        concat_axis=0,
        tiled=True,
        axis_index_groups=[list(range(core, count, 2)) for core in range(2)],
    )
    far = swap(near, "seq", 1)
    acts = dot_nt(factor, weight)
    near, far, acts = lax.optimization_barrier((near, far, acts))
    lower_acts = from_cycle(acts, "rep", 1)
    higher_acts = from_cycle(acts, "rep", -1)

    query_grad, grads, sent = attend(me, queries[0], out_grad[0], log_norm[0], delta, near, far)
    lower_acts, higher_acts, sent = lax.optimization_barrier((lower_acts, higher_acts, sent))

    basis, both = make_basis(acts, lower_acts, higher_acts)
    contrib_parts = []
    last = bits[0]
    for index, bit in enumerate(b for b in reversed(bits) if b != last):
        arrived = swap(sent, "seq", bit)
        share = PARTS - index if bit * 2 == last else 1
        if index < PARTS:
            contrib_parts += [
                contrib_part(both, weight, index + i, PARTS) for i in range(share)
            ]
        both, grads, arrived, contrib_parts = lax.optimization_barrier(
            (both, grads, arrived, contrib_parts)
        )
        grads = grads + arrived.astype(F32)
        keep = grads.shape[0] // 2
        if bit * 2 < last:
            sent = grads[keep:].astype(BF16)
            grads = grads[:keep]
    blocks, grads = lax.optimization_barrier((blocks, grads))
    contrib = jnp.concatenate(contrib_parts, axis=2)
    lower_half = from_cycle(contrib[1], "rep", 1)
    higher_half = from_cycle(contrib[0], "rep", -1)

    upper = (me & last) != 0
    arrived = swap(grads.astype(BF16), "seq", last)
    arrived, lower_half, higher_half = lax.optimization_barrier((arrived, lower_half, higher_half))
    arrived = arrived.astype(F32)
    mine, theirs = grads[:keep], grads[keep:]
    own = jnp.where(upper, mine, mine + arrived[keep:])
    other = jnp.where(upper, theirs + arrived[:keep], arrived[:keep])
    near_b = jnp.concatenate([own, other], axis=0).astype(BF16)
    for bit in bits[1:-1]:
        near_b = jnp.concatenate([near_b, swap(near_b, "seq", bit)], axis=0)
    order = [x // 2 for x in gather_order(count)[: count // 2]]
    proj_mine, proj_theirs = project(me, blocks, near_b, order)
    proj_grad = proj_mine + swap(proj_theirs, "seq", 1)
    right_factor = jnp.stack([contrib[0] + lower_half, contrib[1] + higher_half], axis=0)
    return (
        query_grad[None],
        own[None],
        proj_grad[None],
        basis[None],
        right_factor[None, None],
    )


def solution(mesh):
    return jax.shard_map(
        on_device,
        mesh=mesh,
        in_specs=(
            P("rep", "seq", None),
            P("rep", "seq", None),
            P("rep", "seq", None),
            P("rep", "seq", None),
            P("rep", "seq", None),
            P("rep", None, "seq"),
            P("rep", "seq", None),
            P("rep", "seq", None),
            P("seq", None, None),
        ),
        out_specs=(
            P("rep", "seq", None),
            P("rep", "seq", None),
            P("rep", "seq", None),
            P("rep", None, None, "seq"),
            P("rep", "seq", None, None, None),
        ),
        check_vma=False,
    )
```

```python
import functools
import math

import jax
import jax.numpy as jnp
from jax import lax
from jax.experimental import pallas as pl
from jax.experimental.pallas import tpu as pltpu
from jax.sharding import PartitionSpec as P

WINDOW = 2048
EPSILON = 1e-06
LOG2E = math.log2(math.e)
F32 = jnp.float32
BF16 = jnp.bfloat16
VMEM_LIMIT = 48 * 1024 * 1024
COST = pl.CostEstimate(flops=1, bytes_accessed=1, transcendentals=0)
COST = pl.CostEstimate(flops=1, bytes_accessed=1, transcendentals=0)
COST = pl.CostEstimate(flops=1, bytes_accessed=1, transcendentals=0)


def dot_nt(a, b):
    return lax.dot_general(a, b, (((1,), (1,)), ((), ())), preferred_element_type=F32)


def dot_tn(a, b):
    return lax.dot_general(a, b, (((0,), (0,)), ((), ())), preferred_element_type=F32)


def vmem_specs(count):
    return [pl.BlockSpec(memory_space=pltpu.VMEM)] * count


def local_call(kernel, outs, *args):
    return pl.pallas_call(
        kernel,
        out_shape=outs,
        in_specs=vmem_specs(len(args)),
        out_specs=jax.tree.map(lambda _: pl.BlockSpec(memory_space=pltpu.VMEM), outs),
        cost_estimate=COST,
    )(*args)


def join_kernel(axis, a_ref, b_ref, out_ref):
    cut = a_ref.shape[axis]
    if axis:
        out_ref[:, :cut] = a_ref[...]
        out_ref[:, cut:] = b_ref[...]
    else:
        out_ref[:cut] = a_ref[...]
        out_ref[cut:] = b_ref[...]


def join(a, b, axis=0):
    shape = list(a.shape)
    shape[axis] += b.shape[axis]
    out = jax.ShapeDtypeStruct(shape, a.dtype)
    return local_call(functools.partial(join_kernel, axis), out, a, b)


def add_kernel(kept_ref, arrived_ref, stay_ref, sent_ref):
    total = kept_ref[...] + arrived_ref[...].astype(F32)
    rows = total.shape[0] - sent_ref.shape[0]
    stay_ref[...] = total[: stay_ref.shape[0]]
    sent_ref[...] = total[rows:].astype(BF16)


def add_split(kept, arrived, stay, sent):
    cols = kept.shape[1]
    outs = [jax.ShapeDtypeStruct((stay, cols), F32), jax.ShapeDtypeStruct((sent, cols), BF16)]
    return local_call(add_kernel, outs, kept, arrived)


def merge_kernel(upper_ref, here_ref, there_ref, own_ref, both_ref):
    rows = own_ref.shape[0]
    upper = upper_ref[...] > 0.5
    there = there_ref[...].astype(F32)
    own = jnp.where(upper, here_ref[:rows], here_ref[:rows] + there[rows:])
    other = jnp.where(upper, here_ref[rows:] + there[:rows], there[:rows])
    own_ref[...] = own
    both_ref[:rows] = own.astype(BF16)
    both_ref[rows:] = other.astype(BF16)


def merge(upper, here, there):
    rows, cols = here.shape
    outs = [jax.ShapeDtypeStruct((rows // 2, cols), F32), jax.ShapeDtypeStruct(here.shape, BF16)]
    return local_call(merge_kernel, outs, jnp.full((1, cols), upper, F32), here, there)


def delta_kernel(head_dim, grad_ref, out_ref, delta_ref):
    for head in range(delta_ref.shape[0]):
        cols = slice(head * head_dim, (head + 1) * head_dim)
        prod = grad_ref[:, cols].astype(F32) * out_ref[:, cols].astype(F32)
        delta_ref[head : head + 1, :] = jnp.sum(prod.T, axis=0, keepdims=True)


def head_delta(out_grad, outputs, heads):
    rows, cols = out_grad.shape
    return pl.pallas_call(
        functools.partial(delta_kernel, cols // heads),
        out_shape=jax.ShapeDtypeStruct((heads, rows), F32),
        in_specs=vmem_specs(2),
        out_specs=pl.BlockSpec(memory_space=pltpu.VMEM),
        compiler_params=pltpu.CompilerParams(vmem_limit_bytes=VMEM_LIMIT),
        cost_estimate=COST,
    )(out_grad, outputs)


def swap(block, axis, bit, only_up=None):
    count = lax.axis_size(axis)
    route = [
        (i, i ^ bit) for i in range(count) if only_up is None or (i < i ^ bit) == only_up
    ]
    return lax.ppermute(block, axis, route)


def gather_bits(count):
    return [1 << b for b in reversed(range(count.bit_length() - 1))]


def gather_order(count):
    order = [0]
    for bit in gather_bits(count):
        order = order + [x ^ bit for x in order]
    return order


def swap(block, axis, bit, only_up=None):
    count = lax.axis_size(axis)
    route = [
        (i, i ^ bit) for i in range(count) if only_up is None or (i < i ^ bit) == only_up
    ]
    return lax.ppermute(block, axis, route)


def gather_bits(count):
    return [1 << b for b in reversed(range(count.bit_length() - 1))]


def gather_order(count):
    order = [0]
    for bit in gather_bits(count):
        order = order + [x ^ bit for x in order]
    return order


def attention_kernel(
    order, group, join, scale, me_ref, q_ref, do_ref, norm_ref, delta_ref, near_ref, far_ref,
    qg_ref, near_grad_ref, far_grad_ref, near_t_ref, far_t_ref, qgt_ref,
):
    tok = q_ref.shape[0]
    hd = near_ref.shape[1] // 2
    heads = norm_ref.shape[0]
    half = near_ref.shape[0]
    rows = join * tok
    me = me_ref[0]
    windowed = len(order) * tok > WINDOW
    chunks = [(s, first) for s in range(2) for first in range(0, half, rows)]
    kv_refs = (near_ref, far_ref)
    grad_refs = (near_grad_ref, far_grad_ref)
    t_refs = (near_t_ref, far_t_ref)
    for s, first in chunks:
        t_refs[s][:, first : first + rows] = kv_refs[s][first : first + rows, :hd].T
        grad_refs[s][first : first + rows, :] = jnp.zeros((rows, 2 * hd), F32)

    def step(index, carry):
        def stacked(ref):
            parts = []
            for i in range(group):
                first = pl.multiple_of((index * group + i) * hd, hd)
                parts.append(ref[:, pl.ds(first, hd)])
            return jnp.concatenate(parts, axis=0)

        def row(ref):
            return jnp.concatenate(
                [ref[pl.ds(index * group + i, 1), :] for i in range(group)], axis=1
            )

        q = stacked(q_ref)
        do = stacked(do_ref)
        norm = row(norm_ref) * LOG2E
        delta = row(delta_ref)
        qgt = None
        for s, first in chunks:
            area = slice(first, first + rows)
            key = kv_refs[s][area, :hd]
            value = kv_refs[s][area, hd:]
            logits = dot_nt(key, q) * (scale * LOG2E)
            parts = []
            for j in range(join):
                x = order[(s * half + first) // tok + j]
                source = me ^ x
                part = logits[j * tok : (j + 1) * tok]
                if x == 0 or windowed:
                    key_pos = source * tok + lax.broadcasted_iota(jnp.int32, part.shape, 0)
                    query = lax.broadcasted_iota(jnp.int32, part.shape, 1)
                    query_pos = me * tok + lax.rem(query, tok)
                    visible = (key_pos <= query_pos) & (key_pos > query_pos - WINDOW)
                    parts.append(jnp.where(visible, jnp.exp2(part - norm), 0.0))
                else:
                    hidden = jnp.where(source < me, 0.0, 1e30).astype(F32)
                    parts.append(jnp.exp2(part - (norm + hidden)))
            probs = jnp.concatenate(parts, axis=0)
            prob_grad = dot_nt(value, do)
            score_grad = (scale * probs * (prob_grad - delta)).astype(BF16)
            grad_refs[s][area, hd:] += jnp.dot(
                probs.astype(BF16), do, preferred_element_type=F32
            )
            grad_refs[s][area, :hd] += jnp.dot(score_grad, q, preferred_element_type=F32)
            part = jnp.dot(t_refs[s][:, area], score_grad, preferred_element_type=F32)
            qgt = part if qgt is None else qgt + part
        qgt_ref[...] = qgt
        for i in range(group):
            first = pl.multiple_of((index * group + i) * hd, hd)
            qg_ref[:, pl.ds(first, hd)] = qgt_ref[:, i * tok : (i + 1) * tok].T
        return carry

    lax.fori_loop(0, heads // group, step, 0)


def attend(me, queries, out_grad, norm, delta, near, far):
    tok, cols = queries.shape
    heads = norm.shape[0]
    hd = cols // heads
    half = near.shape[0]
    order = gather_order(2 * half // tok)
    group = next(g for g in (4, 3, 2, 1) if heads % g == 0)
    join = next(j for j in (4, 2, 1) if half % (j * tok) == 0)
    return pl.pallas_call(
        functools.partial(attention_kernel, order, group, join, hd ** (-0.5)),
        out_shape=[
            jax.ShapeDtypeStruct((tok, cols), F32),
            jax.ShapeDtypeStruct((half, 2 * hd), F32),
            jax.ShapeDtypeStruct((half, 2 * hd), F32),
        ],
        in_specs=[pl.BlockSpec(memory_space=pltpu.SMEM)] + vmem_specs(6),
        out_specs=vmem_specs(3),
        scratch_shapes=[
            pltpu.VMEM((hd, half), BF16),
            pltpu.VMEM((hd, half), BF16),
            pltpu.VMEM((hd, group * tok), F32),
        ],
        compiler_params=pltpu.CompilerParams(vmem_limit_bytes=VMEM_LIMIT),
        cost_estimate=COST,
    )(me[None], queries, out_grad, norm, delta, near, far)


def pack_kernel(x_ref, out_ref):
    width = out_ref.shape[2]
    for j in range(out_ref.shape[0]):
        out_ref[j] = x_ref[:, j * width : (j + 1) * width]


def pack(inputs, chips):
    tok, cols = inputs.shape
    return pl.pallas_call(
        pack_kernel,
        out_shape=jax.ShapeDtypeStruct((chips, tok, cols // chips), inputs.dtype),
        in_specs=vmem_specs(1),
        out_specs=pl.BlockSpec(memory_space=pltpu.VMEM),
        compiler_params=pltpu.CompilerParams(vmem_limit_bytes=VMEM_LIMIT),
        cost_estimate=COST,
    )(inputs)


def project_kernel(order, me_ref, x_ref, grads_ref, mine_ref, theirs_ref):
    chip = me_ref[0] // 2
    x = jnp.concatenate([x_ref[chip ^ part] for part in order], axis=0)
    width = mine_ref.shape[0]
    grads = grads_ref[...]
    odd = lax.rem(me_ref[0], 2) == 1
    first = dot_tn(x[:, :width], grads)
    second = dot_tn(x[:, width:], grads)
    mine_ref[...] = jnp.where(odd, second, first)
    theirs_ref[...] = jnp.where(odd, first, second)


def project(me, blocks, grads, order):
    width = blocks.shape[2] // 2
    return pl.pallas_call(
        functools.partial(project_kernel, order),
        out_shape=[jax.ShapeDtypeStruct((width, grads.shape[1]), F32)] * 2,
        in_specs=[pl.BlockSpec(memory_space=pltpu.SMEM)] + vmem_specs(2),
        out_specs=vmem_specs(2),
        compiler_params=pltpu.CompilerParams(vmem_limit_bytes=VMEM_LIMIT),
        cost_estimate=COST,
    )(me[None], blocks, grads)


def orthonormal(rows):
    columns = []
    for source in rows:
        vector = source
        for previous in columns:
            vector = vector - jnp.mean(source * previous, axis=-1, keepdims=True) * previous
        columns.append(
            vector * lax.rsqrt(jnp.mean(vector * vector, axis=-1, keepdims=True) + EPSILON)
        )
    return columns


def basis_kernel(acts_ref, lower_ref, higher_ref, basis_ref, both_ref):
    rank = acts_ref.shape[0]
    rows = [
        acts_ref[k : k + 1]
        - jnp.concatenate([lower_ref[k : k + 1], higher_ref[k : k + 1]], axis=0)
        for k in range(rank)
    ]
    columns = orthonormal(rows)
    edges = [jnp.concatenate([c[e : e + 1] for c in columns], axis=0) for e in range(2)]
    for e, edge in enumerate(edges):
        basis_ref[e] = edge
    both_ref[...] = jnp.concatenate(edges, axis=0).astype(BF16)


def make_basis(acts, lower, higher):
    rank, rows = acts.shape
    return pl.pallas_call(
        basis_kernel,
        out_shape=[
            jax.ShapeDtypeStruct((2, rank, rows), F32),
            jax.ShapeDtypeStruct((2 * rank, rows), BF16),
        ],
        in_specs=vmem_specs(3),
        out_specs=vmem_specs(2),
        cost_estimate=COST,
    )(acts, lower, higher)


def from_cycle(block, axis, distance):
    count = lax.axis_size(axis)
    return lax.ppermute(block, axis, [(i, (i + distance) % count) for i in range(count)])


def on_device(
    queries, keys, values, outputs, out_grad, log_norm, inputs, mlp_weight, initial_right_factor
):
    tok = queries.shape[1]
    heads = log_norm.shape[1]
    count = lax.axis_size("seq")
    me = lax.axis_index("seq")
    bits = gather_bits(count)
    factor = initial_right_factor[0]
    weight = mlp_weight[0]

    near = join(keys[0], values[0], axis=1)
    chips = count // 2
    packed = pack(inputs[0], chips)
    for index, bit in enumerate(bits[:-1]):
        far = swap(near, "seq", bit, True if index == 0 else None)
        if index == 1:
            delta = head_delta(grad_rows, out_rows, heads)
            near, far, delta, packed, factor = lax.optimization_barrier(
                (near, far, delta, packed, factor)
            )
        else:
            near, far, packed, grad_rows, out_rows = lax.optimization_barrier(
                (near, far, packed, out_grad[0], outputs[0])
            )
        near = join(near, far)
    blocks = lax.all_to_all(
        packed,
        "seq",
        split_axis=0,
        concat_axis=0,
        tiled=True,
        axis_index_groups=[list(range(core, count, 2)) for core in range(2)],
    )
    far = swap(near, "seq", 1)
    acts = dot_nt(factor, weight)
    near, far, acts = lax.optimization_barrier((near, far, acts))
    lower_acts = from_cycle(acts, "rep", 1)
    higher_acts = from_cycle(acts, "rep", -1)

    query_grad, grads, sent = attend(me, queries[0], out_grad[0], log_norm[0], delta, near, far)
    lower_acts, higher_acts, sent = lax.optimization_barrier((lower_acts, higher_acts, sent))

    last = bits[0]
    upper = (me & last) != 0
    arrived = swap(sent, "seq", 1)
    basis, both = make_basis(acts, lower_acts, higher_acts)
    contrib = jnp.dot(both, weight, preferred_element_type=F32)
    arrived, contrib, blocks = lax.optimization_barrier((arrived, contrib, blocks))
    contrib = contrib.reshape(2, contrib.shape[0] // 2, contrib.shape[1])
    lower_half = from_cycle(contrib[1], "rep", 1)
    for bit in reversed(bits[1:-1]):
        keep = grads.shape[0] // 2
        grads, sent = add_split(grads, arrived, keep, keep)
        arrived = swap(sent, "seq", bit)
    arrived, lower_half = lax.optimization_barrier((arrived, lower_half))
    higher_half = from_cycle(contrib[0], "rep", -1)

    grads, sent = add_split(grads, arrived, grads.shape[0], grads.shape[0])
    arrived, higher_half = lax.optimization_barrier((swap(sent, "seq", last), higher_half))
    own, near_b = merge(upper.astype(F32), grads, arrived)
    for bit in bits[1:-1]:
        near_b = join(near_b, swap(near_b, "seq", bit))
    order = [x // 2 for x in gather_order(count)[: count // 2]]
    proj_mine, proj_theirs = project(me, blocks, near_b, order)
    proj_grad = proj_mine + swap(proj_theirs, "seq", 1)
    right_factor = jnp.stack([contrib[0] + lower_half, contrib[1] + higher_half], axis=0)
    return (
        query_grad[None],
        own[None],
        proj_grad[None],
        basis[None],
        right_factor[None, None],
    )


def solution(mesh):
    return jax.shard_map(
        on_device,
        mesh=mesh,
        in_specs=(
            P("rep", "seq", None),
            P("rep", "seq", None),
            P("rep", "seq", None),
            P("rep", "seq", None),
            P("rep", "seq", None),
            P("rep", None, "seq"),
            P("rep", "seq", None),
            P("rep", "seq", None),
            P("seq", None, None),
        ),
        out_specs=(
            P("rep", "seq", None),
            P("rep", "seq", None),
            P("rep", "seq", None),
            P("rep", None, None, "seq"),
            P("rep", "seq", None, None, None),
        ),
        check_vma=False,
    )
```

```python
import functools
import math

import jax
import jax.numpy as jnp
from jax import lax
from jax.experimental import pallas as pl
from jax.experimental.pallas import tpu as pltpu
from jax.sharding import PartitionSpec as P

WINDOW = 2048
EPSILON = 1e-06
LOG2E = math.log2(math.e)
F32 = jnp.float32
BF16 = jnp.bfloat16
SMALL = pltpu.CompilerParams(vmem_limit_bytes=8 * 1024 * 1024)
LARGE = pltpu.CompilerParams(vmem_limit_bytes=28 * 1024 * 1024)
COST = pl.CostEstimate(flops=1, bytes_accessed=1, transcendentals=0)
COST = pl.CostEstimate(flops=1, bytes_accessed=1, transcendentals=0)
COST = pl.CostEstimate(flops=1, bytes_accessed=1, transcendentals=0)


def dot_nt(a, b):
    return lax.dot_general(a, b, (((1,), (1,)), ((), ())), preferred_element_type=F32)


def dot_tn(a, b):
    return lax.dot_general(a, b, (((0,), (0,)), ((), ())), preferred_element_type=F32)


def vmem_specs(count):
    return [pl.BlockSpec(memory_space=pltpu.VMEM)] * count


def local_call(kernel, outs, *args):
    return pl.pallas_call(
        kernel,
        out_shape=outs,
        in_specs=vmem_specs(len(args)),
        out_specs=jax.tree.map(lambda _: pl.BlockSpec(memory_space=pltpu.VMEM), outs),
        compiler_params=SMALL,
        cost_estimate=COST,
    )(*args)


def join_kernel(axis, a_ref, b_ref, out_ref):
    cut = a_ref.shape[axis]
    if axis:
        out_ref[:, :cut] = a_ref[...]
        out_ref[:, cut:] = b_ref[...]
    else:
        out_ref[:cut] = a_ref[...]
        out_ref[cut:] = b_ref[...]


def join(a, b, axis=0):
    shape = list(a.shape)
    shape[axis] += b.shape[axis]
    out = jax.ShapeDtypeStruct(shape, a.dtype)
    return local_call(functools.partial(join_kernel, axis), out, a, b)


def add_kernel(kept_ref, arrived_ref, stay_ref, sent_ref):
    total = kept_ref[...] + arrived_ref[...].astype(F32)
    rows = total.shape[0] - sent_ref.shape[0]
    stay_ref[...] = total[: stay_ref.shape[0]]
    sent_ref[...] = total[rows:].astype(BF16)


def add_split(kept, arrived, stay, sent):
    cols = kept.shape[1]
    outs = [jax.ShapeDtypeStruct((stay, cols), F32), jax.ShapeDtypeStruct((sent, cols), BF16)]
    return local_call(add_kernel, outs, kept, arrived)


def merge_kernel(bit, me_ref, here_ref, there_ref, own_ref, both_ref):
    rows = own_ref.shape[0]
    upper = (me_ref[0] & bit) != 0
    there = there_ref[...].astype(F32)
    own = jnp.where(upper, here_ref[:rows], here_ref[:rows] + there[rows:])
    other = jnp.where(upper, here_ref[rows:] + there[:rows], there[:rows])
    own_ref[...] = own
    both_ref[:rows] = own.astype(BF16)
    both_ref[rows:] = other.astype(BF16)


def merge(me, bit, here, there):
    rows, cols = here.shape
    outs = [jax.ShapeDtypeStruct((rows // 2, cols), F32), jax.ShapeDtypeStruct(here.shape, BF16)]
    return pl.pallas_call(
        functools.partial(merge_kernel, bit),
        out_shape=outs,
        in_specs=[pl.BlockSpec(memory_space=pltpu.SMEM)] + vmem_specs(2),
        out_specs=vmem_specs(2),
        compiler_params=SMALL,
        cost_estimate=COST,
    )(me[None], here, there)


def delta_kernel(head_dim, grad_ref, out_ref, delta_ref):
    for head in range(delta_ref.shape[0]):
        cols = slice(head * head_dim, (head + 1) * head_dim)
        prod = grad_ref[:, cols].astype(F32) * out_ref[:, cols].astype(F32)
        delta_ref[head : head + 1, :] = jnp.sum(prod.T, axis=0, keepdims=True)


def head_delta(out_grad, outputs, heads):
    rows, cols = out_grad.shape
    return pl.pallas_call(
        functools.partial(delta_kernel, cols // heads),
        out_shape=jax.ShapeDtypeStruct((heads, rows), F32),
        in_specs=vmem_specs(2),
        out_specs=pl.BlockSpec(memory_space=pltpu.VMEM),
        compiler_params=SMALL,
        cost_estimate=COST,
    )(out_grad, outputs)


def swap(block, axis, bit, only_up=None):
    count = lax.axis_size(axis)
    route = [
        (i, i ^ bit) for i in range(count) if only_up is None or (i < i ^ bit) == only_up
    ]
    return lax.ppermute(block, axis, route)


def gather_bits(count):
    return [1 << b for b in reversed(range(count.bit_length() - 1))]


def gather_order(count):
    order = [0]
    for bit in gather_bits(count):
        order = order + [x ^ bit for x in order]
    return order


def swap(block, axis, bit, only_up=None):
    count = lax.axis_size(axis)
    route = [
        (i, i ^ bit) for i in range(count) if only_up is None or (i < i ^ bit) == only_up
    ]
    return lax.ppermute(block, axis, route)


def gather_bits(count):
    return [1 << b for b in reversed(range(count.bit_length() - 1))]


def gather_order(count):
    order = [0]
    for bit in gather_bits(count):
        order = order + [x ^ bit for x in order]
    return order


def attention_kernel(
    order, group, join, scale, me_ref, q_ref, do_ref, norm_ref, delta_ref, near_ref, far_ref,
    qg_ref, near_grad_ref, far_grad_ref, near_t_ref, far_t_ref, qgt_ref,
):
    tok = q_ref.shape[0]
    hd = near_ref.shape[1] // 2
    heads = norm_ref.shape[0]
    half = near_ref.shape[0]
    rows = join * tok
    me = me_ref[0]
    windowed = len(order) * tok > WINDOW
    chunks = [(s, first) for s in range(2) for first in range(0, half, rows)]
    kv_refs = (near_ref, far_ref)
    grad_refs = (near_grad_ref, far_grad_ref)
    t_refs = (near_t_ref, far_t_ref)
    for s, first in chunks:
        t_refs[s][:, first : first + rows] = kv_refs[s][first : first + rows, :hd].T
        grad_refs[s][first : first + rows, :] = jnp.zeros((rows, 2 * hd), F32)

    def step(index, carry):
        def stacked(ref):
            parts = []
            for i in range(group):
                first = pl.multiple_of((index * group + i) * hd, hd)
                parts.append(ref[:, pl.ds(first, hd)])
            return jnp.concatenate(parts, axis=0)

        def row(ref):
            return jnp.concatenate(
                [ref[pl.ds(index * group + i, 1), :] for i in range(group)], axis=1
            )

        q = stacked(q_ref)
        do = stacked(do_ref)
        norm = row(norm_ref) * LOG2E
        delta = row(delta_ref)
        qgt = None
        for s, first in chunks:
            area = slice(first, first + rows)
            key = kv_refs[s][area, :hd]
            value = kv_refs[s][area, hd:]
            logits = dot_nt(key, q) * (scale * LOG2E)
            parts = []
            for j in range(join):
                x = order[(s * half + first) // tok + j]
                source = me ^ x
                part = logits[j * tok : (j + 1) * tok]
                if x == 0 or windowed:
                    key_pos = source * tok + lax.broadcasted_iota(jnp.int32, part.shape, 0)
                    query = lax.broadcasted_iota(jnp.int32, part.shape, 1)
                    query_pos = me * tok + lax.rem(query, tok)
                    visible = (key_pos <= query_pos) & (key_pos > query_pos - WINDOW)
                    parts.append(jnp.where(visible, jnp.exp2(part - norm), 0.0))
                else:
                    hidden = jnp.where(source < me, 0.0, 1e30).astype(F32)
                    parts.append(jnp.exp2(part - (norm + hidden)))
            probs = jnp.concatenate(parts, axis=0)
            prob_grad = dot_nt(value, do)
            score_grad = (scale * probs * (prob_grad - delta)).astype(BF16)
            grad_refs[s][area, hd:] += jnp.dot(
                probs.astype(BF16), do, preferred_element_type=F32
            )
            grad_refs[s][area, :hd] += jnp.dot(score_grad, q, preferred_element_type=F32)
            part = jnp.dot(t_refs[s][:, area], score_grad, preferred_element_type=F32)
            qgt = part if qgt is None else qgt + part
        qgt_ref[...] = qgt
        for i in range(group):
            first = pl.multiple_of((index * group + i) * hd, hd)
            qg_ref[:, pl.ds(first, hd)] = qgt_ref[:, i * tok : (i + 1) * tok].T
        return carry

    lax.fori_loop(0, heads // group, step, 0)


def attend(me, queries, out_grad, norm, delta, near, far):
    tok, cols = queries.shape
    heads = norm.shape[0]
    hd = cols // heads
    half = near.shape[0]
    order = gather_order(2 * half // tok)
    group = next(g for g in (4, 3, 2, 1) if heads % g == 0)
    join = next(j for j in (4, 2, 1) if half % (j * tok) == 0)
    return pl.pallas_call(
        functools.partial(attention_kernel, order, group, join, hd ** (-0.5)),
        out_shape=[
            jax.ShapeDtypeStruct((tok, cols), F32),
            jax.ShapeDtypeStruct((half, 2 * hd), F32),
            jax.ShapeDtypeStruct((half, 2 * hd), F32),
        ],
        in_specs=[pl.BlockSpec(memory_space=pltpu.SMEM)] + vmem_specs(6),
        out_specs=vmem_specs(3),
        scratch_shapes=[
            pltpu.VMEM((hd, half), BF16),
            pltpu.VMEM((hd, half), BF16),
            pltpu.VMEM((hd, group * tok), F32),
        ],
        compiler_params=LARGE,
        cost_estimate=COST,
    )(me[None], queries, out_grad, norm, delta, near, far)


def pack_kernel(x_ref, out_ref):
    width = out_ref.shape[2]
    for j in range(out_ref.shape[0]):
        out_ref[j] = x_ref[:, j * width : (j + 1) * width]


def pack(inputs, chips):
    tok, cols = inputs.shape
    return pl.pallas_call(
        pack_kernel,
        out_shape=jax.ShapeDtypeStruct((chips, tok, cols // chips), inputs.dtype),
        in_specs=vmem_specs(1),
        out_specs=pl.BlockSpec(memory_space=pltpu.VMEM),
        compiler_params=SMALL,
        cost_estimate=COST,
    )(inputs)


def project_kernel(order, me_ref, x_ref, grads_ref, mine_ref, theirs_ref):
    chip = me_ref[0] // 2
    x = jnp.concatenate([x_ref[chip ^ part] for part in order], axis=0)
    width = mine_ref.shape[0]
    grads = grads_ref[...]
    odd = lax.rem(me_ref[0], 2) == 1
    first = dot_tn(x[:, :width], grads)
    second = dot_tn(x[:, width:], grads)
    mine_ref[...] = jnp.where(odd, second, first)
    theirs_ref[...] = jnp.where(odd, first, second)


def project(me, blocks, grads, order):
    width = blocks.shape[2] // 2
    return pl.pallas_call(
        functools.partial(project_kernel, order),
        out_shape=[jax.ShapeDtypeStruct((width, grads.shape[1]), F32)] * 2,
        in_specs=[pl.BlockSpec(memory_space=pltpu.SMEM)] + vmem_specs(2),
        out_specs=vmem_specs(2),
        compiler_params=LARGE,
        cost_estimate=COST,
    )(me[None], blocks, grads)


def orthonormal(rows):
    columns = []
    for source in rows:
        vector = source
        for previous in columns:
            vector = vector - jnp.mean(source * previous, axis=-1, keepdims=True) * previous
        columns.append(
            vector * lax.rsqrt(jnp.mean(vector * vector, axis=-1, keepdims=True) + EPSILON)
        )
    return columns


def basis_kernel(acts_ref, lower_ref, higher_ref, basis_ref, both_ref):
    rank = acts_ref.shape[0]
    rows = [
        acts_ref[k : k + 1]
        - jnp.concatenate([lower_ref[k : k + 1], higher_ref[k : k + 1]], axis=0)
        for k in range(rank)
    ]
    columns = orthonormal(rows)
    edges = [jnp.concatenate([c[e : e + 1] for c in columns], axis=0) for e in range(2)]
    for e, edge in enumerate(edges):
        basis_ref[e] = edge
    both_ref[...] = jnp.concatenate(edges, axis=0).astype(BF16)


def make_basis(acts, lower, higher):
    rank, rows = acts.shape
    return pl.pallas_call(
        basis_kernel,
        out_shape=[
            jax.ShapeDtypeStruct((2, rank, rows), F32),
            jax.ShapeDtypeStruct((2 * rank, rows), BF16),
        ],
        in_specs=vmem_specs(3),
        out_specs=vmem_specs(2),
        compiler_params=SMALL,
        cost_estimate=COST,
    )(acts, lower, higher)


def from_cycle(block, axis, distance):
    count = lax.axis_size(axis)
    return lax.ppermute(block, axis, [(i, (i + distance) % count) for i in range(count)])


def on_device(
    queries, keys, values, outputs, out_grad, log_norm, inputs, mlp_weight, initial_right_factor
):
    tok = queries.shape[1]
    heads = log_norm.shape[1]
    count = lax.axis_size("seq")
    me = lax.axis_index("seq")
    bits = gather_bits(count)
    factor = initial_right_factor[0]
    weight = mlp_weight[0]

    near = join(keys[0], values[0], axis=1)
    chips = count // 2
    packed = pack(inputs[0], chips)
    for index, bit in enumerate(bits[:-1]):
        far = swap(near, "seq", bit, True if index == 0 else None)
        if index == 1:
            delta = head_delta(grad_rows, out_rows, heads)
            near, far, delta, packed, factor = lax.optimization_barrier(
                (near, far, delta, packed, factor)
            )
        else:
            near, far, packed, grad_rows, out_rows = lax.optimization_barrier(
                (near, far, packed, out_grad[0], outputs[0])
            )
        near = join(near, far)
    blocks = lax.all_to_all(
        packed,
        "seq",
        split_axis=0,
        concat_axis=0,
        tiled=True,
        axis_index_groups=[list(range(core, count, 2)) for core in range(2)],
    )
    far = swap(near, "seq", 1)
    acts = dot_nt(factor, weight)
    near, far, acts = lax.optimization_barrier((near, far, acts))
    lower_acts = from_cycle(acts, "rep", 1)
    higher_acts = from_cycle(acts, "rep", -1)

    query_grad, grads, sent = attend(me, queries[0], out_grad[0], log_norm[0], delta, near, far)
    lower_acts, higher_acts, sent = lax.optimization_barrier((lower_acts, higher_acts, sent))

    last = bits[0]
    arrived = swap(sent, "seq", 1)
    basis, both = make_basis(acts, lower_acts, higher_acts)
    contrib = jnp.dot(both, weight, preferred_element_type=F32)
    arrived, contrib, blocks = lax.optimization_barrier((arrived, contrib, blocks))
    contrib = contrib.reshape(2, contrib.shape[0] // 2, contrib.shape[1])
    lower_half = from_cycle(contrib[1], "rep", 1)
    for bit in reversed(bits[1:-1]):
        keep = grads.shape[0] // 2
        grads, sent = add_split(grads, arrived, keep, keep)
        arrived = swap(sent, "seq", bit)
    higher_half = from_cycle(contrib[0], "rep", -1)

    grads, sent = add_split(grads, arrived, grads.shape[0], grads.shape[0])
    arrived = swap(sent, "seq", last)
    own, near_b = merge(me, last, grads, arrived)
    for bit in bits[1:-1]:
        near_b = join(near_b, swap(near_b, "seq", bit))
    order = [x // 2 for x in gather_order(count)[: count // 2]]
    proj_mine, proj_theirs = project(me, blocks, near_b, order)
    proj_grad = proj_mine + swap(proj_theirs, "seq", 1)
    right_factor = jnp.stack([contrib[0] + lower_half, contrib[1] + higher_half], axis=0)
    return (
        query_grad[None],
        own[None],
        proj_grad[None],
        basis[None],
        right_factor[None, None],
    )


def solution(mesh):
    return jax.shard_map(
        on_device,
        mesh=mesh,
        in_specs=(
            P("rep", "seq", None),
            P("rep", "seq", None),
            P("rep", "seq", None),
            P("rep", "seq", None),
            P("rep", "seq", None),
            P("rep", None, "seq"),
            P("rep", "seq", None),
            P("rep", "seq", None),
            P("seq", None, None),
        ),
        out_specs=(
            P("rep", "seq", None),
            P("rep", "seq", None),
            P("rep", "seq", None),
            P("rep", None, None, "seq"),
            P("rep", "seq", None, None, None),
        ),
        check_vma=False,
    )
```

```python
import functools
import math

import jax
import jax.numpy as jnp
from jax import lax
from jax.experimental import pallas as pl
from jax.experimental.pallas import tpu as pltpu
from jax.sharding import PartitionSpec as P

WINDOW = 2048
EPSILON = 1e-06
LOG2E = math.log2(math.e)
F32 = jnp.float32
BF16 = jnp.bfloat16
SMALL = pltpu.CompilerParams(vmem_limit_bytes=8 * 1024 * 1024)
LARGE = pltpu.CompilerParams(vmem_limit_bytes=28 * 1024 * 1024)
COST = pl.CostEstimate(flops=1, bytes_accessed=1, transcendentals=0)
COST = pl.CostEstimate(flops=1, bytes_accessed=1, transcendentals=0)
COST = pl.CostEstimate(flops=1, bytes_accessed=1, transcendentals=0)


def dot_nt(a, b):
    return lax.dot_general(a, b, (((1,), (1,)), ((), ())), preferred_element_type=F32)


def dot_tn(a, b):
    return lax.dot_general(a, b, (((0,), (0,)), ((), ())), preferred_element_type=F32)


def vmem_specs(count):
    return [pl.BlockSpec(memory_space=pltpu.VMEM)] * count


def local_call(kernel, outs, *args):
    return pl.pallas_call(
        kernel,
        out_shape=outs,
        in_specs=vmem_specs(len(args)),
        out_specs=jax.tree.map(lambda _: pl.BlockSpec(memory_space=pltpu.VMEM), outs),
        compiler_params=SMALL,
        cost_estimate=COST,
    )(*args)


def join_kernel(a_ref, b_ref, out_ref):
    rows = a_ref.shape[0]
    out_ref[:rows] = a_ref[...]
    out_ref[rows:] = b_ref[...]


def join(a, b):
    out = jax.ShapeDtypeStruct((a.shape[0] + b.shape[0], a.shape[1]), a.dtype)
    return local_call(join_kernel, out, a, b)


def add_kernel(kept_ref, arrived_ref, stay_ref, sent_ref):
    total = kept_ref[...] + arrived_ref[...].astype(F32)
    rows = total.shape[0] - sent_ref.shape[0]
    stay_ref[...] = total[: stay_ref.shape[0]]
    sent_ref[...] = total[rows:].astype(BF16)


def add_split(kept, arrived, stay, sent):
    cols = kept.shape[1]
    outs = [jax.ShapeDtypeStruct((stay, cols), F32), jax.ShapeDtypeStruct((sent, cols), BF16)]
    return local_call(add_kernel, outs, kept, arrived)


def merge_kernel(bit, me_ref, here_ref, there_ref, own_ref, both_ref):
    rows = own_ref.shape[0]
    upper = (me_ref[0] & bit) != 0
    there = there_ref[...].astype(F32)
    own = jnp.where(upper, here_ref[:rows], here_ref[:rows] + there[rows:])
    other = jnp.where(upper, here_ref[rows:] + there[:rows], there[:rows])
    own_ref[...] = own
    both_ref[:rows] = own.astype(BF16)
    both_ref[rows:] = other.astype(BF16)


def merge(me, bit, here, there):
    rows, cols = here.shape
    outs = [jax.ShapeDtypeStruct((rows // 2, cols), F32), jax.ShapeDtypeStruct(here.shape, BF16)]
    return pl.pallas_call(
        functools.partial(merge_kernel, bit),
        out_shape=outs,
        in_specs=[pl.BlockSpec(memory_space=pltpu.SMEM)] + vmem_specs(2),
        out_specs=vmem_specs(2),
        compiler_params=SMALL,
        cost_estimate=COST,
    )(me[None], here, there)


def delta_kernel(head_dim, grad_ref, out_ref, delta_ref):
    for head in range(delta_ref.shape[0]):
        cols = slice(head * head_dim, (head + 1) * head_dim)
        prod = grad_ref[:, cols].astype(F32) * out_ref[:, cols].astype(F32)
        delta_ref[head : head + 1, :] = jnp.sum(prod.T, axis=0, keepdims=True)


def head_delta(out_grad, outputs, heads):
    rows, cols = out_grad.shape
    return pl.pallas_call(
        functools.partial(delta_kernel, cols // heads),
        out_shape=jax.ShapeDtypeStruct((heads, rows), F32),
        in_specs=vmem_specs(2),
        out_specs=pl.BlockSpec(memory_space=pltpu.VMEM),
        compiler_params=SMALL,
        cost_estimate=COST,
    )(out_grad, outputs)


def swap(block, axis, bit, only_up=None):
    count = lax.axis_size(axis)
    route = [
        (i, i ^ bit) for i in range(count) if only_up is None or (i < i ^ bit) == only_up
    ]
    return lax.ppermute(block, axis, route)


def gather_bits(count):
    return [1 << b for b in reversed(range(count.bit_length() - 1))]


def gather_order(count):
    order = [0]
    for bit in gather_bits(count):
        order = order + [x ^ bit for x in order]
    return order


def swap(block, axis, bit, only_up=None):
    count = lax.axis_size(axis)
    route = [
        (i, i ^ bit) for i in range(count) if only_up is None or (i < i ^ bit) == only_up
    ]
    return lax.ppermute(block, axis, route)


def gather_bits(count):
    return [1 << b for b in reversed(range(count.bit_length() - 1))]


def gather_order(count):
    order = [0]
    for bit in gather_bits(count):
        order = order + [x ^ bit for x in order]
    return order


def attention_kernel(
    order, group, join, scale, me_ref, q_ref, do_ref, norm_ref, delta_ref, near_ref, far_ref,
    qg_ref, near_grad_ref, far_grad_ref, near_t_ref, far_t_ref, qgt_ref,
):
    tok = q_ref.shape[0]
    hd = near_ref.shape[1] // 2
    heads = norm_ref.shape[0]
    half = near_ref.shape[0]
    rows = join * tok
    me = me_ref[0]
    windowed = len(order) * tok > WINDOW
    chunks = [(s, first) for s in range(2) for first in range(0, half, rows)]
    kv_refs = (near_ref, far_ref)
    grad_refs = (near_grad_ref, far_grad_ref)
    t_refs = (near_t_ref, far_t_ref)
    for s, first in chunks:
        t_refs[s][:, first : first + rows] = kv_refs[s][first : first + rows, :hd].T
        grad_refs[s][first : first + rows, :] = jnp.zeros((rows, 2 * hd), F32)

    def step(index, carry):
        def stacked(ref):
            parts = []
            for i in range(group):
                first = pl.multiple_of((index * group + i) * hd, hd)
                parts.append(ref[:, pl.ds(first, hd)])
            return jnp.concatenate(parts, axis=0)

        def row(ref):
            return jnp.concatenate(
                [ref[pl.ds(index * group + i, 1), :] for i in range(group)], axis=1
            )

        q = stacked(q_ref)
        do = stacked(do_ref)
        norm = row(norm_ref) * LOG2E
        delta = row(delta_ref)
        qgt = None
        for s, first in chunks:
            area = slice(first, first + rows)
            key = kv_refs[s][area, :hd]
            value = kv_refs[s][area, hd:]
            logits = dot_nt(key, q) * (scale * LOG2E)
            parts = []
            for j in range(join):
                x = order[(s * half + first) // tok + j]
                source = me ^ x
                part = logits[j * tok : (j + 1) * tok]
                if x == 0 or windowed:
                    key_pos = source * tok + lax.broadcasted_iota(jnp.int32, part.shape, 0)
                    query = lax.broadcasted_iota(jnp.int32, part.shape, 1)
                    query_pos = me * tok + lax.rem(query, tok)
                    visible = (key_pos <= query_pos) & (key_pos > query_pos - WINDOW)
                    parts.append(jnp.where(visible, jnp.exp2(part - norm), 0.0))
                else:
                    hidden = jnp.where(source < me, 0.0, 1e30).astype(F32)
                    parts.append(jnp.exp2(part - (norm + hidden)))
            probs = jnp.concatenate(parts, axis=0)
            prob_grad = dot_nt(value, do)
            score_grad = (scale * probs * (prob_grad - delta)).astype(BF16)
            grad_refs[s][area, hd:] += jnp.dot(
                probs.astype(BF16), do, preferred_element_type=F32
            )
            grad_refs[s][area, :hd] += jnp.dot(score_grad, q, preferred_element_type=F32)
            part = jnp.dot(t_refs[s][:, area], score_grad, preferred_element_type=F32)
            qgt = part if qgt is None else qgt + part
        qgt_ref[...] = qgt
        for i in range(group):
            first = pl.multiple_of((index * group + i) * hd, hd)
            qg_ref[:, pl.ds(first, hd)] = qgt_ref[:, i * tok : (i + 1) * tok].T
        return carry

    lax.fori_loop(0, heads // group, step, 0)


def attend(me, queries, out_grad, norm, delta, near, far):
    tok, cols = queries.shape
    heads = norm.shape[0]
    hd = cols // heads
    half = near.shape[0]
    order = gather_order(2 * half // tok)
    group = next(g for g in (4, 3, 2, 1) if heads % g == 0)
    join = next(j for j in (4, 2, 1) if half % (j * tok) == 0)
    return pl.pallas_call(
        functools.partial(attention_kernel, order, group, join, hd ** (-0.5)),
        out_shape=[
            jax.ShapeDtypeStruct((tok, cols), F32),
            jax.ShapeDtypeStruct((half, 2 * hd), F32),
            jax.ShapeDtypeStruct((half, 2 * hd), F32),
        ],
        in_specs=[pl.BlockSpec(memory_space=pltpu.SMEM)] + vmem_specs(6),
        out_specs=vmem_specs(3),
        scratch_shapes=[
            pltpu.VMEM((hd, half), BF16),
            pltpu.VMEM((hd, half), BF16),
            pltpu.VMEM((hd, group * tok), F32),
        ],
        compiler_params=LARGE,
        cost_estimate=COST,
    )(me[None], queries, out_grad, norm, delta, near, far)


def pack_kernel(x_ref, out_ref):
    width = out_ref.shape[2]
    for j in range(out_ref.shape[0]):
        out_ref[j] = x_ref[:, j * width : (j + 1) * width]


def pack(inputs, chips):
    tok, cols = inputs.shape
    return pl.pallas_call(
        pack_kernel,
        out_shape=jax.ShapeDtypeStruct((chips, tok, cols // chips), inputs.dtype),
        in_specs=vmem_specs(1),
        out_specs=pl.BlockSpec(memory_space=pltpu.VMEM),
        compiler_params=SMALL,
        cost_estimate=COST,
    )(inputs)


def project_kernel(order, me_ref, x_ref, grads_ref, mine_ref, theirs_ref):
    chip = me_ref[0] // 2
    x = jnp.concatenate([x_ref[chip ^ part] for part in order], axis=0)
    width = mine_ref.shape[0]
    grads = grads_ref[...]
    odd = lax.rem(me_ref[0], 2) == 1
    first = dot_tn(x[:, :width], grads)
    second = dot_tn(x[:, width:], grads)
    mine_ref[...] = jnp.where(odd, second, first)
    theirs_ref[...] = jnp.where(odd, first, second)


def project(me, blocks, grads, order):
    width = blocks.shape[2] // 2
    return pl.pallas_call(
        functools.partial(project_kernel, order),
        out_shape=[jax.ShapeDtypeStruct((width, grads.shape[1]), F32)] * 2,
        in_specs=[pl.BlockSpec(memory_space=pltpu.SMEM)] + vmem_specs(2),
        out_specs=vmem_specs(2),
        compiler_params=LARGE,
        cost_estimate=COST,
    )(me[None], blocks, grads)


def orthonormal(rows):
    columns = []
    for source in rows:
        vector = source
        for previous in columns:
            vector = vector - jnp.mean(source * previous, axis=-1, keepdims=True) * previous
        columns.append(
            vector * lax.rsqrt(jnp.mean(vector * vector, axis=-1, keepdims=True) + EPSILON)
        )
    return columns


def basis_kernel(acts_ref, lower_ref, higher_ref, basis_ref, both_ref):
    rank = acts_ref.shape[0]
    rows = [
        acts_ref[k : k + 1]
        - jnp.concatenate([lower_ref[k : k + 1], higher_ref[k : k + 1]], axis=0)
        for k in range(rank)
    ]
    columns = orthonormal(rows)
    edges = [jnp.concatenate([c[e : e + 1] for c in columns], axis=0) for e in range(2)]
    for e, edge in enumerate(edges):
        basis_ref[e] = edge
    both_ref[...] = jnp.concatenate(edges, axis=0).astype(BF16)


def make_basis(acts, lower, higher):
    rank, rows = acts.shape
    return pl.pallas_call(
        basis_kernel,
        out_shape=[
            jax.ShapeDtypeStruct((2, rank, rows), F32),
            jax.ShapeDtypeStruct((2 * rank, rows), BF16),
        ],
        in_specs=vmem_specs(3),
        out_specs=vmem_specs(2),
        compiler_params=SMALL,
        cost_estimate=COST,
    )(acts, lower, higher)


def from_cycle(block, axis, distance):
    count = lax.axis_size(axis)
    return lax.ppermute(block, axis, [(i, (i + distance) % count) for i in range(count)])


def on_device(
    queries, keys, values, outputs, out_grad, log_norm, inputs, mlp_weight, initial_right_factor
):
    tok = queries.shape[1]
    heads = log_norm.shape[1]
    count = lax.axis_size("seq")
    me = lax.axis_index("seq")
    bits = gather_bits(count)
    factor = initial_right_factor[0]
    weight = mlp_weight[0]

    near = jnp.concatenate([keys[0], values[0]], axis=-1)
    chips = count // 2
    packed = pack(inputs[0], chips)
    for index, bit in enumerate(bits[:-1]):
        far = swap(near, "seq", bit, True if index == 0 else None)
        if index == 1:
            delta = head_delta(grad_rows, out_rows, heads)
            near, far, delta, packed, factor = lax.optimization_barrier(
                (near, far, delta, packed, factor)
            )
        else:
            near, far, packed, grad_rows, out_rows = lax.optimization_barrier(
                (near, far, packed, out_grad[0], outputs[0])
            )
        near, packed = lax.optimization_barrier((join(near, far), packed))
    blocks = lax.all_to_all(
        packed,
        "seq",
        split_axis=0,
        concat_axis=0,
        tiled=True,
        axis_index_groups=[list(range(core, count, 2)) for core in range(2)],
    )
    far = swap(near, "seq", 1)
    acts = dot_nt(factor, weight)
    near, far, acts = lax.optimization_barrier((near, far, acts))
    lower_acts = from_cycle(acts, "rep", 1)
    higher_acts = from_cycle(acts, "rep", -1)

    query_grad, grads, sent = attend(me, queries[0], out_grad[0], log_norm[0], delta, near, far)
    lower_acts, higher_acts, sent = lax.optimization_barrier((lower_acts, higher_acts, sent))

    last = bits[0]
    half = weight.shape[1] // 2
    arrived = swap(sent, "seq", 1)
    basis, both = make_basis(acts, lower_acts, higher_acts)
    arrived, basis, both = lax.optimization_barrier((arrived, basis, both))
    contrib = None
    for bit in reversed(bits[1:-1]):
        keep = grads.shape[0] // 2
        grads, sent = add_split(grads, arrived, keep, keep)
        arrived = swap(sent, "seq", bit)
        if contrib is None:
            contrib = jnp.dot(both, weight[:, :half], preferred_element_type=F32)
            arrived, contrib, both, blocks = lax.optimization_barrier(
                (arrived, contrib, both, blocks)
            )

    grads, sent = add_split(grads, arrived, grads.shape[0], grads.shape[0])
    arrived = swap(sent, "seq", last)
    if contrib is None:
        contrib = jnp.dot(both, weight[:, :half], preferred_element_type=F32)
    rest = jnp.dot(both, weight[:, half:], preferred_element_type=F32)
    arrived, rest = lax.optimization_barrier((arrived, rest))
    contrib = jnp.concatenate([contrib, rest], axis=1)
    contrib = contrib.reshape(2, contrib.shape[0] // 2, contrib.shape[1])
    lower_half = from_cycle(contrib[1], "rep", 1)
    higher_half = from_cycle(contrib[0], "rep", -1)
    own, near_b = merge(me, last, grads, arrived)
    for bit in bits[1:-1]:
        near_b = join(near_b, swap(near_b, "seq", bit))
    order = [x // 2 for x in gather_order(count)[: count // 2]]
    proj_mine, proj_theirs = project(me, blocks, near_b, order)
    proj_grad = proj_mine + swap(proj_theirs, "seq", 1)
    right_factor = jnp.stack([contrib[0] + lower_half, contrib[1] + higher_half], axis=0)
    return (
        query_grad[None],
        own[None],
        proj_grad[None],
        basis[None],
        right_factor[None, None],
    )


def solution(mesh):
    return jax.shard_map(
        on_device,
        mesh=mesh,
        in_specs=(
            P("rep", "seq", None),
            P("rep", "seq", None),
            P("rep", "seq", None),
            P("rep", "seq", None),
            P("rep", "seq", None),
            P("rep", None, "seq"),
            P("rep", "seq", None),
            P("rep", "seq", None),
            P("seq", None, None),
        ),
        out_specs=(
            P("rep", "seq", None),
            P("rep", "seq", None),
            P("rep", "seq", None),
            P("rep", None, None, "seq"),
            P("rep", "seq", None, None, None),
        ),
        check_vma=False,
    )
```

```python
import functools
import math

import jax
import jax.numpy as jnp
from jax import lax
from jax.experimental import pallas as pl
from jax.experimental.pallas import tpu as pltpu
from jax.sharding import PartitionSpec as P

WINDOW = 2048
EPSILON = 1e-06
LOG2E = math.log2(math.e)
F32 = jnp.float32
BF16 = jnp.bfloat16
SMALL = pltpu.CompilerParams(vmem_limit_bytes=8 * 1024 * 1024)
LARGE = pltpu.CompilerParams(vmem_limit_bytes=28 * 1024 * 1024)
COST = pl.CostEstimate(flops=1, bytes_accessed=1, transcendentals=0)
COST = pl.CostEstimate(flops=1, bytes_accessed=1, transcendentals=0)
COST = pl.CostEstimate(flops=1, bytes_accessed=1, transcendentals=0)


def dot_nt(a, b):
    return lax.dot_general(a, b, (((1,), (1,)), ((), ())), preferred_element_type=F32)


def dot_tn(a, b):
    return lax.dot_general(a, b, (((0,), (0,)), ((), ())), preferred_element_type=F32)


def vmem_specs(count):
    return [pl.BlockSpec(memory_space=pltpu.VMEM)] * count


def local_call(kernel, outs, *args):
    return pl.pallas_call(
        kernel,
        out_shape=outs,
        in_specs=vmem_specs(len(args)),
        out_specs=jax.tree.map(lambda _: pl.BlockSpec(memory_space=pltpu.VMEM), outs),
        compiler_params=SMALL,
        cost_estimate=COST,
    )(*args)


def join_kernel(a_ref, b_ref, out_ref):
    rows = a_ref.shape[0]
    out_ref[:rows] = a_ref[...]
    out_ref[rows:] = b_ref[...]


def join(a, b):
    out = jax.ShapeDtypeStruct((a.shape[0] + b.shape[0], a.shape[1]), a.dtype)
    return local_call(join_kernel, out, a, b)


def add_kernel(kept_ref, arrived_ref, stay_ref, sent_ref):
    total = kept_ref[...] + arrived_ref[...].astype(F32)
    rows = total.shape[0] - sent_ref.shape[0]
    stay_ref[...] = total[: stay_ref.shape[0]]
    sent_ref[...] = total[rows:].astype(BF16)


def add_split(kept, arrived, stay, sent):
    cols = kept.shape[1]
    outs = [jax.ShapeDtypeStruct((stay, cols), F32), jax.ShapeDtypeStruct((sent, cols), BF16)]
    return local_call(add_kernel, outs, kept, arrived)


def merge_kernel(bit, me_ref, here_ref, there_ref, own_ref, both_ref):
    rows = own_ref.shape[0]
    upper = (me_ref[0] & bit) != 0
    there = there_ref[...].astype(F32)
    own = jnp.where(upper, here_ref[:rows], here_ref[:rows] + there[rows:])
    other = jnp.where(upper, here_ref[rows:] + there[:rows], there[:rows])
    own_ref[...] = own
    both_ref[:rows] = own.astype(BF16)
    both_ref[rows:] = other.astype(BF16)


def merge(me, bit, here, there):
    rows, cols = here.shape
    outs = [jax.ShapeDtypeStruct((rows // 2, cols), F32), jax.ShapeDtypeStruct(here.shape, BF16)]
    return pl.pallas_call(
        functools.partial(merge_kernel, bit),
        out_shape=outs,
        in_specs=[pl.BlockSpec(memory_space=pltpu.SMEM)] + vmem_specs(2),
        out_specs=vmem_specs(2),
        compiler_params=SMALL,
        cost_estimate=COST,
    )(me[None], here, there)


def delta_kernel(head_dim, grad_ref, out_ref, delta_ref):
    for head in range(delta_ref.shape[0]):
        cols = slice(head * head_dim, (head + 1) * head_dim)
        prod = grad_ref[:, cols].astype(F32) * out_ref[:, cols].astype(F32)
        delta_ref[head : head + 1, :] = jnp.sum(prod.T, axis=0, keepdims=True)


def head_delta(out_grad, outputs, heads):
    rows, cols = out_grad.shape
    return pl.pallas_call(
        functools.partial(delta_kernel, cols // heads),
        out_shape=jax.ShapeDtypeStruct((heads, rows), F32),
        in_specs=vmem_specs(2),
        out_specs=pl.BlockSpec(memory_space=pltpu.VMEM),
        compiler_params=SMALL,
        cost_estimate=COST,
    )(out_grad, outputs)


def swap(block, axis, bit, only_up=None):
    count = lax.axis_size(axis)
    route = [
        (i, i ^ bit) for i in range(count) if only_up is None or (i < i ^ bit) == only_up
    ]
    return lax.ppermute(block, axis, route)


def gather_bits(count):
    return [1 << b for b in reversed(range(count.bit_length() - 1))]


def gather_order(count):
    order = [0]
    for bit in gather_bits(count):
        order = order + [x ^ bit for x in order]
    return order


def swap(block, axis, bit, only_up=None):
    count = lax.axis_size(axis)
    route = [
        (i, i ^ bit) for i in range(count) if only_up is None or (i < i ^ bit) == only_up
    ]
    return lax.ppermute(block, axis, route)


def gather_bits(count):
    return [1 << b for b in reversed(range(count.bit_length() - 1))]


def gather_order(count):
    order = [0]
    for bit in gather_bits(count):
        order = order + [x ^ bit for x in order]
    return order


def attention_kernel(
    order, group, join, scale, me_ref, q_ref, do_ref, norm_ref, delta_ref, near_ref, far_ref,
    qg_ref, near_grad_ref, far_grad_ref, near_t_ref, far_t_ref, qgt_ref,
):
    tok = q_ref.shape[0]
    hd = near_ref.shape[1] // 2
    heads = norm_ref.shape[0]
    half = near_ref.shape[0]
    rows = join * tok
    me = me_ref[0]
    windowed = len(order) * tok > WINDOW
    chunks = [(s, first) for s in range(2) for first in range(0, half, rows)]
    kv_refs = (near_ref, far_ref)
    grad_refs = (near_grad_ref, far_grad_ref)
    t_refs = (near_t_ref, far_t_ref)
    for s, first in chunks:
        t_refs[s][:, first : first + rows] = kv_refs[s][first : first + rows, :hd].T
        grad_refs[s][first : first + rows, :] = jnp.zeros((rows, 2 * hd), F32)

    def step(index, carry):
        def stacked(ref):
            parts = []
            for i in range(group):
                first = pl.multiple_of((index * group + i) * hd, hd)
                parts.append(ref[:, pl.ds(first, hd)])
            return jnp.concatenate(parts, axis=0)

        def row(ref):
            return jnp.concatenate(
                [ref[pl.ds(index * group + i, 1), :] for i in range(group)], axis=1
            )

        q = stacked(q_ref)
        do = stacked(do_ref)
        norm = row(norm_ref) * LOG2E
        delta = row(delta_ref)
        qgt = None
        for s, first in chunks:
            area = slice(first, first + rows)
            key = kv_refs[s][area, :hd]
            value = kv_refs[s][area, hd:]
            logits = dot_nt(key, q) * (scale * LOG2E)
            parts = []
            for j in range(join):
                x = order[(s * half + first) // tok + j]
                source = me ^ x
                part = logits[j * tok : (j + 1) * tok]
                if x == 0 or windowed:
                    key_pos = source * tok + lax.broadcasted_iota(jnp.int32, part.shape, 0)
                    query = lax.broadcasted_iota(jnp.int32, part.shape, 1)
                    query_pos = me * tok + lax.rem(query, tok)
                    visible = (key_pos <= query_pos) & (key_pos > query_pos - WINDOW)
                    parts.append(jnp.where(visible, jnp.exp2(part - norm), 0.0))
                else:
                    hidden = jnp.where(source < me, 0.0, 1e30).astype(F32)
                    parts.append(jnp.exp2(part - (norm + hidden)))
            probs = jnp.concatenate(parts, axis=0)
            prob_grad = dot_nt(value, do)
            score_grad = (scale * probs * (prob_grad - delta)).astype(BF16)
            grad_refs[s][area, hd:] += jnp.dot(
                probs.astype(BF16), do, preferred_element_type=F32
            )
            grad_refs[s][area, :hd] += jnp.dot(score_grad, q, preferred_element_type=F32)
            part = jnp.dot(t_refs[s][:, area], score_grad, preferred_element_type=F32)
            qgt = part if qgt is None else qgt + part
        qgt_ref[...] = qgt
        for i in range(group):
            first = pl.multiple_of((index * group + i) * hd, hd)
            qg_ref[:, pl.ds(first, hd)] = qgt_ref[:, i * tok : (i + 1) * tok].T
        return carry

    lax.fori_loop(0, heads // group, step, 0)


def attend(me, queries, out_grad, norm, delta, near, far):
    tok, cols = queries.shape
    heads = norm.shape[0]
    hd = cols // heads
    half = near.shape[0]
    order = gather_order(2 * half // tok)
    group = next(g for g in (4, 3, 2, 1) if heads % g == 0)
    join = next(j for j in (4, 2, 1) if half % (j * tok) == 0)
    return pl.pallas_call(
        functools.partial(attention_kernel, order, group, join, hd ** (-0.5)),
        out_shape=[
            jax.ShapeDtypeStruct((tok, cols), F32),
            jax.ShapeDtypeStruct((half, 2 * hd), F32),
            jax.ShapeDtypeStruct((half, 2 * hd), F32),
        ],
        in_specs=[pl.BlockSpec(memory_space=pltpu.SMEM)] + vmem_specs(6),
        out_specs=vmem_specs(3),
        scratch_shapes=[
            pltpu.VMEM((hd, half), BF16),
            pltpu.VMEM((hd, half), BF16),
            pltpu.VMEM((hd, group * tok), F32),
        ],
        compiler_params=LARGE,
        cost_estimate=COST,
    )(me[None], queries, out_grad, norm, delta, near, far)


def pack_kernel(x_ref, out_ref):
    width = out_ref.shape[2]
    for j in range(out_ref.shape[0]):
        out_ref[j] = x_ref[:, j * width : (j + 1) * width]


def pack(inputs, chips):
    tok, cols = inputs.shape
    return pl.pallas_call(
        pack_kernel,
        out_shape=jax.ShapeDtypeStruct((chips, tok, cols // chips), inputs.dtype),
        in_specs=vmem_specs(1),
        out_specs=pl.BlockSpec(memory_space=pltpu.VMEM),
        compiler_params=SMALL,
        cost_estimate=COST,
    )(inputs)


def project_kernel(order, me_ref, x_ref, grads_ref, mine_ref, theirs_ref):
    chip = me_ref[0] // 2
    x = jnp.concatenate([x_ref[chip ^ part] for part in order], axis=0)
    width = mine_ref.shape[0]
    grads = grads_ref[...]
    odd = lax.rem(me_ref[0], 2) == 1
    first = dot_tn(x[:, :width], grads)
    second = dot_tn(x[:, width:], grads)
    mine_ref[...] = jnp.where(odd, second, first)
    theirs_ref[...] = jnp.where(odd, first, second)


def project(me, blocks, grads, order):
    width = blocks.shape[2] // 2
    return pl.pallas_call(
        functools.partial(project_kernel, order),
        out_shape=[jax.ShapeDtypeStruct((width, grads.shape[1]), F32)] * 2,
        in_specs=[pl.BlockSpec(memory_space=pltpu.SMEM)] + vmem_specs(2),
        out_specs=vmem_specs(2),
        compiler_params=LARGE,
        cost_estimate=COST,
    )(me[None], blocks, grads)


def orthonormal(rows):
    columns = []
    for source in rows:
        vector = source
        for previous in columns:
            vector = vector - jnp.mean(source * previous, axis=-1, keepdims=True) * previous
        columns.append(
            vector * lax.rsqrt(jnp.mean(vector * vector, axis=-1, keepdims=True) + EPSILON)
        )
    return columns


def basis_kernel(acts_ref, lower_ref, higher_ref, basis_ref, both_ref):
    rank = acts_ref.shape[0]
    rows = [
        acts_ref[k : k + 1]
        - jnp.concatenate([lower_ref[k : k + 1], higher_ref[k : k + 1]], axis=0)
        for k in range(rank)
    ]
    columns = orthonormal(rows)
    edges = [jnp.concatenate([c[e : e + 1] for c in columns], axis=0) for e in range(2)]
    for e, edge in enumerate(edges):
        basis_ref[e] = edge
    both_ref[...] = jnp.concatenate(edges, axis=0).astype(BF16)


def make_basis(acts, lower, higher):
    rank, rows = acts.shape
    return pl.pallas_call(
        basis_kernel,
        out_shape=[
            jax.ShapeDtypeStruct((2, rank, rows), F32),
            jax.ShapeDtypeStruct((2 * rank, rows), BF16),
        ],
        in_specs=vmem_specs(3),
        out_specs=vmem_specs(2),
        compiler_params=SMALL,
        cost_estimate=COST,
    )(acts, lower, higher)


def from_cycle(block, axis, distance):
    count = lax.axis_size(axis)
    return lax.ppermute(block, axis, [(i, (i + distance) % count) for i in range(count)])


def on_device(
    queries, keys, values, outputs, out_grad, log_norm, inputs, mlp_weight, initial_right_factor
):
    tok = queries.shape[1]
    heads = log_norm.shape[1]
    count = lax.axis_size("seq")
    me = lax.axis_index("seq")
    bits = gather_bits(count)
    factor = initial_right_factor[0]
    weight = mlp_weight[0]

    near = jnp.concatenate([keys[0], values[0]], axis=-1)
    chips = count // 2
    packed = pack(inputs[0], chips)
    for index, bit in enumerate(bits[:-1]):
        far = swap(near, "seq", bit, True if index == 0 else None)
        if index == 1:
            delta = head_delta(grad_rows, out_rows, heads)
            near, far, delta, packed, factor = lax.optimization_barrier(
                (near, far, delta, packed, factor)
            )
        else:
            near, far, packed, grad_rows, out_rows = lax.optimization_barrier(
                (near, far, packed, out_grad[0], outputs[0])
            )
        near, packed = lax.optimization_barrier((join(near, far), packed))
    blocks = lax.all_to_all(
        packed,
        "seq",
        split_axis=0,
        concat_axis=0,
        tiled=True,
        axis_index_groups=[list(range(core, count, 2)) for core in range(2)],
    )
    far = swap(near, "seq", 1)
    acts = dot_nt(factor, weight)
    near, far, acts = lax.optimization_barrier((near, far, acts))
    lower_acts = from_cycle(acts, "rep", 1)
    higher_acts = from_cycle(acts, "rep", -1)

    query_grad, grads, sent = attend(me, queries[0], out_grad[0], log_norm[0], delta, near, far)
    lower_acts, higher_acts, sent = lax.optimization_barrier((lower_acts, higher_acts, sent))

    last = bits[0]
    arrived = swap(sent, "seq", 1)
    basis, both = make_basis(acts, lower_acts, higher_acts)
    arrived, basis, both = lax.optimization_barrier((arrived, basis, both))
    contrib = None
    for bit in reversed(bits[1:-1]):
        keep = grads.shape[0] // 2
        grads, sent = add_split(grads, arrived, keep, keep)
        arrived = swap(sent, "seq", bit)
        if contrib is None:
            contrib = jnp.dot(both, weight, preferred_element_type=F32)
            arrived, contrib, blocks = lax.optimization_barrier((arrived, contrib, blocks))

    grads, sent = add_split(grads, arrived, grads.shape[0], grads.shape[0])
    arrived = swap(sent, "seq", last)
    if contrib is None:
        contrib = jnp.dot(both, weight, preferred_element_type=F32)
    contrib = contrib.reshape(2, contrib.shape[0] // 2, contrib.shape[1])
    lower_half = from_cycle(contrib[1], "rep", 1)
    higher_half = from_cycle(contrib[0], "rep", -1)
    own, near_b = merge(me, last, grads, arrived)
    for bit in bits[1:-1]:
        near_b = join(near_b, swap(near_b, "seq", bit))
    order = [x // 2 for x in gather_order(count)[: count // 2]]
    proj_mine, proj_theirs = project(me, blocks, near_b, order)
    proj_grad = proj_mine + swap(proj_theirs, "seq", 1)
    right_factor = jnp.stack([contrib[0] + lower_half, contrib[1] + higher_half], axis=0)
    return (
        query_grad[None],
        own[None],
        proj_grad[None],
        basis[None],
        right_factor[None, None],
    )


def solution(mesh):
    return jax.shard_map(
        on_device,
        mesh=mesh,
        in_specs=(
            P("rep", "seq", None),
            P("rep", "seq", None),
            P("rep", "seq", None),
            P("rep", "seq", None),
            P("rep", "seq", None),
            P("rep", None, "seq"),
            P("rep", "seq", None),
            P("rep", "seq", None),
            P("seq", None, None),
        ),
        out_specs=(
            P("rep", "seq", None),
            P("rep", "seq", None),
            P("rep", "seq", None),
            P("rep", None, None, "seq"),
            P("rep", "seq", None, None, None),
        ),
        check_vma=False,
    )
```

```python
import functools
import math

import jax
import jax.numpy as jnp
from jax import lax
from jax.experimental import pallas as pl
from jax.experimental.pallas import tpu as pltpu
from jax.sharding import PartitionSpec as P

WINDOW = 2048
EPSILON = 1e-06
LOG2E = math.log2(math.e)
F32 = jnp.float32
BF16 = jnp.bfloat16
SMALL = pltpu.CompilerParams(vmem_limit_bytes=8 * 1024 * 1024)
LARGE = pltpu.CompilerParams(vmem_limit_bytes=28 * 1024 * 1024)
COST = pl.CostEstimate(flops=1, bytes_accessed=1, transcendentals=0)
COST = pl.CostEstimate(flops=1, bytes_accessed=1, transcendentals=0)
COST = pl.CostEstimate(flops=1, bytes_accessed=1, transcendentals=0)


def dot_nt(a, b):
    return lax.dot_general(a, b, (((1,), (1,)), ((), ())), preferred_element_type=F32)


def dot_tn(a, b):
    return lax.dot_general(a, b, (((0,), (0,)), ((), ())), preferred_element_type=F32)


def vmem_specs(count):
    return [pl.BlockSpec(memory_space=pltpu.VMEM)] * count


def local_call(kernel, outs, *args):
    return pl.pallas_call(
        kernel,
        out_shape=outs,
        in_specs=vmem_specs(len(args)),
        out_specs=jax.tree.map(lambda _: pl.BlockSpec(memory_space=pltpu.VMEM), outs),
        compiler_params=SMALL,
        cost_estimate=COST,
    )(*args)


def join_kernel(a_ref, b_ref, out_ref):
    rows = a_ref.shape[0]
    out_ref[:rows] = a_ref[...]
    out_ref[rows:] = b_ref[...]


def join(a, b):
    out = jax.ShapeDtypeStruct((a.shape[0] + b.shape[0], a.shape[1]), a.dtype)
    return local_call(join_kernel, out, a, b)


def add_kernel(kept_ref, arrived_ref, stay_ref, sent_ref):
    total = kept_ref[...] + arrived_ref[...].astype(F32)
    rows = total.shape[0] - sent_ref.shape[0]
    stay_ref[...] = total[: stay_ref.shape[0]]
    sent_ref[...] = total[rows:].astype(BF16)


def add_split(kept, arrived, stay, sent):
    cols = kept.shape[1]
    outs = [jax.ShapeDtypeStruct((stay, cols), F32), jax.ShapeDtypeStruct((sent, cols), BF16)]
    return local_call(add_kernel, outs, kept, arrived)


def merge_kernel(bit, me_ref, here_ref, there_ref, own_ref, both_ref):
    rows = own_ref.shape[0]
    upper = (me_ref[0] & bit) != 0
    there = there_ref[...].astype(F32)
    own = jnp.where(upper, here_ref[:rows], here_ref[:rows] + there[rows:])
    other = jnp.where(upper, here_ref[rows:] + there[:rows], there[:rows])
    own_ref[...] = own
    both_ref[:rows] = own.astype(BF16)
    both_ref[rows:] = other.astype(BF16)


def merge(me, bit, here, there):
    rows, cols = here.shape
    outs = [jax.ShapeDtypeStruct((rows // 2, cols), F32), jax.ShapeDtypeStruct(here.shape, BF16)]
    return pl.pallas_call(
        functools.partial(merge_kernel, bit),
        out_shape=outs,
        in_specs=[pl.BlockSpec(memory_space=pltpu.SMEM)] + vmem_specs(2),
        out_specs=vmem_specs(2),
        compiler_params=SMALL,
        cost_estimate=COST,
    )(me[None], here, there)


def delta_kernel(head_dim, grad_ref, out_ref, delta_ref):
    for head in range(delta_ref.shape[0]):
        cols = slice(head * head_dim, (head + 1) * head_dim)
        prod = grad_ref[:, cols].astype(F32) * out_ref[:, cols].astype(F32)
        delta_ref[head : head + 1, :] = jnp.sum(prod.T, axis=0, keepdims=True)


def head_delta(out_grad, outputs, heads):
    rows, cols = out_grad.shape
    return pl.pallas_call(
        functools.partial(delta_kernel, cols // heads),
        out_shape=jax.ShapeDtypeStruct((heads, rows), F32),
        in_specs=vmem_specs(2),
        out_specs=pl.BlockSpec(memory_space=pltpu.VMEM),
        compiler_params=SMALL,
        cost_estimate=COST,
    )(out_grad, outputs)


def swap(block, axis, bit, only_up=None):
    count = lax.axis_size(axis)
    route = [
        (i, i ^ bit) for i in range(count) if only_up is None or (i < i ^ bit) == only_up
    ]
    return lax.ppermute(block, axis, route)


def gather_bits(count):
    return [1 << b for b in reversed(range(count.bit_length() - 1))]


def gather_order(count):
    order = [0]
    for bit in gather_bits(count):
        order = order + [x ^ bit for x in order]
    return order


def swap(block, axis, bit, only_up=None):
    count = lax.axis_size(axis)
    route = [
        (i, i ^ bit) for i in range(count) if only_up is None or (i < i ^ bit) == only_up
    ]
    return lax.ppermute(block, axis, route)


def gather_bits(count):
    return [1 << b for b in reversed(range(count.bit_length() - 1))]


def gather_order(count):
    order = [0]
    for bit in gather_bits(count):
        order = order + [x ^ bit for x in order]
    return order


def attention_kernel(
    order, group, join, scale, me_ref, q_ref, do_ref, norm_ref, delta_ref, near_ref, far_ref,
    qg_ref, near_grad_ref, far_grad_ref, near_t_ref, far_t_ref, qgt_ref,
):
    tok = q_ref.shape[0]
    hd = near_ref.shape[1] // 2
    heads = norm_ref.shape[0]
    half = near_ref.shape[0]
    rows = join * tok
    me = me_ref[0]
    windowed = len(order) * tok > WINDOW
    chunks = [(s, first) for s in range(2) for first in range(0, half, rows)]
    kv_refs = (near_ref, far_ref)
    grad_refs = (near_grad_ref, far_grad_ref)
    t_refs = (near_t_ref, far_t_ref)
    for s, first in chunks:
        t_refs[s][:, first : first + rows] = kv_refs[s][first : first + rows, :hd].T
        grad_refs[s][first : first + rows, :] = jnp.zeros((rows, 2 * hd), F32)

    def step(index, carry):
        def stacked(ref):
            parts = []
            for i in range(group):
                first = pl.multiple_of((index * group + i) * hd, hd)
                parts.append(ref[:, pl.ds(first, hd)])
            return jnp.concatenate(parts, axis=0)

        def row(ref):
            return jnp.concatenate(
                [ref[pl.ds(index * group + i, 1), :] for i in range(group)], axis=1
            )

        q = stacked(q_ref)
        do = stacked(do_ref)
        norm = row(norm_ref) * LOG2E
        delta = row(delta_ref)
        qgt = None
        for s, first in chunks:
            area = slice(first, first + rows)
            key = kv_refs[s][area, :hd]
            value = kv_refs[s][area, hd:]
            logits = dot_nt(key, q) * (scale * LOG2E)
            parts = []
            for j in range(join):
                x = order[(s * half + first) // tok + j]
                source = me ^ x
                part = logits[j * tok : (j + 1) * tok]
                if x == 0 or windowed:
                    key_pos = source * tok + lax.broadcasted_iota(jnp.int32, part.shape, 0)
                    query = lax.broadcasted_iota(jnp.int32, part.shape, 1)
                    query_pos = me * tok + lax.rem(query, tok)
                    visible = (key_pos <= query_pos) & (key_pos > query_pos - WINDOW)
                    parts.append(jnp.where(visible, jnp.exp2(part - norm), 0.0))
                else:
                    hidden = jnp.where(source < me, 0.0, 1e30).astype(F32)
                    parts.append(jnp.exp2(part - (norm + hidden)))
            probs = jnp.concatenate(parts, axis=0)
            prob_grad = dot_nt(value, do)
            score_grad = (scale * probs * (prob_grad - delta)).astype(BF16)
            grad_refs[s][area, hd:] += jnp.dot(
                probs.astype(BF16), do, preferred_element_type=F32
            )
            grad_refs[s][area, :hd] += jnp.dot(score_grad, q, preferred_element_type=F32)
            part = jnp.dot(t_refs[s][:, area], score_grad, preferred_element_type=F32)
            qgt = part if qgt is None else qgt + part
        qgt_ref[...] = qgt
        for i in range(group):
            first = pl.multiple_of((index * group + i) * hd, hd)
            qg_ref[:, pl.ds(first, hd)] = qgt_ref[:, i * tok : (i + 1) * tok].T
        return carry

    lax.fori_loop(0, heads // group, step, 0)


def attend(me, queries, out_grad, norm, delta, near, far):
    tok, cols = queries.shape
    heads = norm.shape[0]
    hd = cols // heads
    half = near.shape[0]
    order = gather_order(2 * half // tok)
    group = next(g for g in (4, 3, 2, 1) if heads % g == 0)
    join = next(j for j in (4, 2, 1) if half % (j * tok) == 0)
    return pl.pallas_call(
        functools.partial(attention_kernel, order, group, join, hd ** (-0.5)),
        out_shape=[
            jax.ShapeDtypeStruct((tok, cols), F32),
            jax.ShapeDtypeStruct((half, 2 * hd), F32),
            jax.ShapeDtypeStruct((half, 2 * hd), F32),
        ],
        in_specs=[pl.BlockSpec(memory_space=pltpu.SMEM)] + vmem_specs(6),
        out_specs=vmem_specs(3),
        scratch_shapes=[
            pltpu.VMEM((hd, half), BF16),
            pltpu.VMEM((hd, half), BF16),
            pltpu.VMEM((hd, group * tok), F32),
        ],
        compiler_params=LARGE,
        cost_estimate=COST,
    )(me[None], queries, out_grad, norm, delta, near, far)


def pack_kernel(x_ref, out_ref):
    width = out_ref.shape[2]
    for j in range(out_ref.shape[0]):
        out_ref[j] = x_ref[:, j * width : (j + 1) * width]


def pack(inputs, chips):
    tok, cols = inputs.shape
    return pl.pallas_call(
        pack_kernel,
        out_shape=jax.ShapeDtypeStruct((chips, tok, cols // chips), inputs.dtype),
        in_specs=vmem_specs(1),
        out_specs=pl.BlockSpec(memory_space=pltpu.VMEM),
        compiler_params=SMALL,
        cost_estimate=COST,
    )(inputs)


def project_kernel(order, me_ref, x_ref, grads_ref, mine_ref, theirs_ref):
    chip = me_ref[0] // 2
    x = jnp.concatenate([x_ref[chip ^ part] for part in order], axis=0)
    width = mine_ref.shape[0]
    grads = grads_ref[...]
    odd = lax.rem(me_ref[0], 2) == 1
    first = dot_tn(x[:, :width], grads)
    second = dot_tn(x[:, width:], grads)
    mine_ref[...] = jnp.where(odd, second, first)
    theirs_ref[...] = jnp.where(odd, first, second)


def project(me, blocks, grads, order):
    width = blocks.shape[2] // 2
    return pl.pallas_call(
        functools.partial(project_kernel, order),
        out_shape=[jax.ShapeDtypeStruct((width, grads.shape[1]), F32)] * 2,
        in_specs=[pl.BlockSpec(memory_space=pltpu.SMEM)] + vmem_specs(2),
        out_specs=vmem_specs(2),
        compiler_params=LARGE,
        cost_estimate=COST,
    )(me[None], blocks, grads)


def orthonormal(rows):
    columns = []
    for source in rows:
        vector = source
        for previous in columns:
            vector = vector - jnp.mean(source * previous, axis=-1, keepdims=True) * previous
        columns.append(
            vector * lax.rsqrt(jnp.mean(vector * vector, axis=-1, keepdims=True) + EPSILON)
        )
    return columns


def basis_kernel(acts_ref, lower_ref, higher_ref, basis_ref, both_ref):
    rank = acts_ref.shape[0]
    rows = [
        acts_ref[k : k + 1]
        - jnp.concatenate([lower_ref[k : k + 1], higher_ref[k : k + 1]], axis=0)
        for k in range(rank)
    ]
    columns = orthonormal(rows)
    edges = [jnp.concatenate([c[e : e + 1] for c in columns], axis=0) for e in range(2)]
    for e, edge in enumerate(edges):
        basis_ref[e] = edge
    both_ref[...] = jnp.concatenate(edges, axis=0).astype(BF16)


def make_basis(acts, lower, higher):
    rank, rows = acts.shape
    return pl.pallas_call(
        basis_kernel,
        out_shape=[
            jax.ShapeDtypeStruct((2, rank, rows), F32),
            jax.ShapeDtypeStruct((2 * rank, rows), BF16),
        ],
        in_specs=vmem_specs(3),
        out_specs=vmem_specs(2),
        compiler_params=SMALL,
        cost_estimate=COST,
    )(acts, lower, higher)


def from_cycle(block, axis, distance):
    count = lax.axis_size(axis)
    return lax.ppermute(block, axis, [(i, (i + distance) % count) for i in range(count)])


def on_device(
    queries, keys, values, outputs, out_grad, log_norm, inputs, mlp_weight, initial_right_factor
):
    tok = queries.shape[1]
    heads = log_norm.shape[1]
    count = lax.axis_size("seq")
    me = lax.axis_index("seq")
    bits = gather_bits(count)
    factor = initial_right_factor[0]
    weight = mlp_weight[0]

    near = jnp.concatenate([keys[0], values[0]], axis=-1)
    chips = count // 2
    packed = pack(inputs[0], chips)
    for index, bit in enumerate(bits[:-1]):
        far = swap(near, "seq", bit, True if index == 0 else None)
        if index == 1:
            delta = head_delta(grad_rows, out_rows, heads)
            near, far, delta, packed, factor = lax.optimization_barrier(
                (near, far, delta, packed, factor)
            )
        else:
            near, far, packed, grad_rows, out_rows = lax.optimization_barrier(
                (near, far, packed, out_grad[0], outputs[0])
            )
        near, packed = lax.optimization_barrier((join(near, far), packed))
    blocks = lax.all_to_all(
        packed,
        "seq",
        split_axis=0,
        concat_axis=0,
        tiled=True,
        axis_index_groups=[list(range(core, count, 2)) for core in range(2)],
    )
    far = swap(near, "seq", 1)
    acts = dot_nt(factor, weight)
    near, far, acts = lax.optimization_barrier((near, far, acts))
    lower_acts = from_cycle(acts, "rep", 1)
    higher_acts = from_cycle(acts, "rep", -1)

    query_grad, grads, sent = attend(me, queries[0], out_grad[0], log_norm[0], delta, near, far)
    lower_acts, higher_acts, sent = lax.optimization_barrier((lower_acts, higher_acts, sent))

    last = bits[0]
    arrived = swap(sent, "seq", 1)
    basis, both = make_basis(acts, lower_acts, higher_acts)
    arrived, basis, both = lax.optimization_barrier((arrived, basis, both))
    contrib = None
    for bit in reversed(bits[1:-1]):
        keep = grads.shape[0] // 2
        grads, sent = add_split(grads, arrived, keep, keep)
        arrived = swap(sent, "seq", bit)
        if contrib is None:
            contrib = jnp.dot(both, weight, preferred_element_type=F32)
            arrived, contrib, blocks = lax.optimization_barrier((arrived, contrib, blocks))

    if contrib is None:
        contrib = jnp.dot(both, weight, preferred_element_type=F32)
    contrib = contrib.reshape(2, contrib.shape[0] // 2, contrib.shape[1])
    lower_half = from_cycle(contrib[1], "rep", 1)
    higher_half = from_cycle(contrib[0], "rep", -1)

    grads, sent = add_split(grads, arrived, grads.shape[0], grads.shape[0])
    arrived = swap(sent, "seq", last)
    arrived, lower_half, higher_half = lax.optimization_barrier((arrived, lower_half, higher_half))
    own, near_b = merge(me, last, grads, arrived)
    for bit in bits[1:-1]:
        near_b = join(near_b, swap(near_b, "seq", bit))
    order = [x // 2 for x in gather_order(count)[: count // 2]]
    proj_mine, proj_theirs = project(me, blocks, near_b, order)
    proj_grad = proj_mine + swap(proj_theirs, "seq", 1)
    right_factor = jnp.stack([contrib[0] + lower_half, contrib[1] + higher_half], axis=0)
    return (
        query_grad[None],
        own[None],
        proj_grad[None],
        basis[None],
        right_factor[None, None],
    )


def solution(mesh):
    return jax.shard_map(
        on_device,
        mesh=mesh,
        in_specs=(
            P("rep", "seq", None),
            P("rep", "seq", None),
            P("rep", "seq", None),
            P("rep", "seq", None),
            P("rep", "seq", None),
            P("rep", None, "seq"),
            P("rep", "seq", None),
            P("rep", "seq", None),
            P("seq", None, None),
        ),
        out_specs=(
            P("rep", "seq", None),
            P("rep", "seq", None),
            P("rep", "seq", None),
            P("rep", None, None, "seq"),
            P("rep", "seq", None, None, None),
        ),
        check_vma=False,
    )
```
